128 devices in a mesh: grp: 4 (over z), ctx: 32 (over y, x, core).
Axes of the slice: x: 4, y: 4, z: 4, core: 2. Of those that a mesh axis runs over, the one named last changes fastest.
Arguments:
- block_input: bfloat16 [8, 2048, 1024], P('grp', 'ctx'), may hold values from -6 to 6
- seq_lengths: int32 [8], P('grp'), may hold values from 256 to 2048, as said below
- in_gain: bfloat16 [1024], P('grp'), may hold values from 0.099609375 to 1.8984375
- w_mixer: bfloat16 [1024, 4096], P('grp'), may hold values from -0.1875 to 0.1875
- conv_weight: bfloat16 [4, 4096], P(None, 'grp'), may hold values from -3 to 3
- w_rates: bfloat16 [1024, 16], P('grp'), may hold values from -1 to 1
- decay_scale: bfloat16 [8], P('grp'), may hold values from -3 to 3
- decay_bias: bfloat16 [8], P('grp'), may hold values from -7 to -2
- w_outgate: bfloat16 [1024, 2048], P('grp'), may hold values from -0.1875 to 0.1875
- head_gain: bfloat16 [256], P('grp'), may hold values from 0.099609375 to 1.8984375
- w_output: bfloat16 [2048, 1024], P('grp'), may hold values from -0.1875 to 0.1875
- mlp_gain: bfloat16 [1024], P('grp'), may hold values from 0.099609375 to 1.8984375
- w_gateup: bfloat16 [1024, 5632], P('grp'), may hold values from -0.1875 to 0.1875
- w_down: bfloat16 [2816, 1024], P('grp'), may hold values from -0.15625 to 0.15625
- cotangent: bfloat16 [8, 2048, 1024], P('grp', 'ctx'), may hold values from -6 to 6
Outputs:
- block_output: bfloat16 [8, 2048, 1024], P('grp', 'ctx')
- input_grad: float32 [8, 2048, 1024], P('grp', 'ctx')
- grad_in_gain: float32 [1024], P('grp')
- grad_mixer: float32 [1024, 4096], P('grp')
- grad_conv: float32 [4, 4096], P(None, 'grp')
- grad_rates: float32 [1024, 16], P('grp')
- grad_decay_scale: float32 [8], P('grp')
- grad_decay_bias: float32 [8], P('grp')
- grad_outgate: float32 [1024, 2048], P('grp')
- grad_head_gain: float32 [256], P('grp')
- grad_output: float32 [2048, 1024], P('grp')
- grad_mlp_gain: float32 [1024], P('grp')
- grad_gateup: float32 [1024, 5632], P('grp')
- grad_down: float32 [2816, 1024], P('grp')
The draws below stay inside these ranges and needn't reach their ends.
Inputs may be any that keep to these rules, and one draw needn't show every extreme that they name: `seq_lengths`: of each 2 consecutive sequences one, chosen by the seed, has all 2048 slots valid.
All inputs are finite; a program needn't handle non-finite values.
Results may differ from the reference program's by a relative error of at most 0.011.
The reference program's roundings to bfloat16 on the way count: a program that leaves them out, or rounds other values in their place, can miss the bound.
Values may be sent and summed in bfloat16 or wider, within the bound.
No kernel may reach another device: no remote copies, remote signals or barrier semaphores. Data moves between devices by JAX's collectives and lax.ppermute only.
A program may use at most 576 MiB of HBM per device.

```python
import jax
import jax.numpy as jnp
from jax import lax

D = 1024
HEADS = 8
KEY_DIM = 128
VALUE_DIM = 256
FF = 2816
CONV = 4
SPAN = 64
SEQS = 2
LENGTH = 2048
SEQUENCES = 8


def common_offset(key):
    return 0.5 * jnp.clip(jax.random.normal(jax.random.fold_in(key, 101), (D,), jnp.float32), -4.0, 4.0)


def chosen_heads(key, count):
    order = jax.random.permutation(jax.random.fold_in(key, 202), HEADS)
    return order < count


def draw_seq_lengths(key, part):
    key = jax.random.fold_in(key, 17)
    pick_key, length_key = jax.random.split(key)
    groups = SEQUENCES // SEQS
    chosen = jax.random.randint(pick_key, (groups, 1), 0, SEQS)
    others = jax.random.randint(length_key, (groups, SEQS), LENGTH // 8, LENGTH + 1)
    slots = jnp.arange(SEQS, dtype=jnp.int32)[None, :]
    return jnp.where(slots == chosen, LENGTH, others).reshape(SEQUENCES).astype(jnp.int32)


def draw_block_input(key, part):
    offset = common_offset(key)
    noise_key = jax.random.fold_in(key, 11)
    noise = jnp.clip(jax.random.normal(noise_key, (SEQUENCES, LENGTH, D), jnp.float32), -4.0, 4.0)
    return (noise + offset[None, None, :]).astype(jnp.bfloat16)


def draw_w_rates(key, part):
    offset = common_offset(key)
    noise_key = jax.random.fold_in(key, 13)
    picked = chosen_heads(key, HEADS // 2)
    noise = jnp.clip(jax.random.normal(noise_key, (D, 2 * HEADS), jnp.float32), -4.0, 4.0)
    noise = noise * D ** (-0.5)
    shifted = -15.65 * offset / D
    write_cols = noise[:, :HEADS] + jnp.where(picked[None, :], shifted[:, None], 0.0)
    return jnp.concatenate([write_cols, noise[:, HEADS:]], axis=1).astype(jnp.bfloat16)


def draw_decay_scale(key, part):
    slow_key = jax.random.fold_in(key, 23)
    fast_key = jax.random.fold_in(key, 29)
    picked = chosen_heads(key, HEADS // 2)
    slow_values = jax.random.uniform(slow_key, (HEADS,), jnp.float32, -3.0, -2.0)
    fast_values = jax.random.uniform(fast_key, (HEADS,), jnp.float32, 0.0, 3.0)
    return jnp.where(picked, slow_values, fast_values).astype(jnp.bfloat16)


def draw_decay_bias(key, part):
    slow_key = jax.random.fold_in(key, 31)
    fast_key = jax.random.fold_in(key, 37)
    picked = chosen_heads(key, HEADS // 2)
    slow_values = jax.random.uniform(slow_key, (HEADS,), jnp.float32, -7.0, -6.0)
    fast_values = jax.random.uniform(fast_key, (HEADS,), jnp.float32, -7.0, -2.0)
    return jnp.where(picked, slow_values, fast_values).astype(jnp.bfloat16)


def level_of(own_key, dims, cuts, smallest, top_value):
    level = 1.0
    for dim, parts in cuts:
        heights = jax.random.uniform(jax.random.fold_in(jax.random.fold_in(own_key, 6), dim), (parts,), jnp.float32, smallest / len(cuts), top_value / len(cuts))
        level = level * jnp.repeat(jnp.exp(heights), dims[dim] // parts).reshape((-1,) + (1,) * (len(dims) - 1 - dim))
    return level


def scatter_about(stream_key, dims, scale, bound, shards=(), held_as=jnp.bfloat16):
    values = scale * jax.random.normal(stream_key, dims, jnp.float32)
    if shards:
        values = values * level_of(stream_key, dims, shards, -0.22, 0.18)
    return jnp.clip(values, -bound, bound).astype(held_as)


def setup_inputs(seed: int = 0) -> dict:
    splits = jax.random.split(jax.random.key(seed), 16)
    return {
        "block_input": draw_block_input(jax.random.fold_in(splits[15], 71), 0),
        "seq_lengths": draw_seq_lengths(jax.random.fold_in(splits[15], 71), 0),
        "in_gain": jnp.clip(1.0 + 0.18 * jax.random.normal(splits[2], (D,), jnp.float32), 0.099609375, 1.8984375).astype(jnp.bfloat16),
        "w_mixer": scatter_about(splits[3], (D, 2 * HEADS * KEY_DIM + HEADS * VALUE_DIM), D ** -0.5, 0.1875, ((0, 4),)),
        "conv_weight": scatter_about(splits[4], (CONV, 2 * HEADS * KEY_DIM + HEADS * VALUE_DIM), 0.5, 3.0, ((1, 4),)),
        "w_rates": draw_w_rates(jax.random.fold_in(splits[15], 71), 0),
        "decay_scale": draw_decay_scale(jax.random.fold_in(splits[15], 71), 0),
        "decay_bias": draw_decay_bias(jax.random.fold_in(splits[15], 71), 0),
        "w_outgate": scatter_about(splits[8], (D, HEADS * VALUE_DIM), D ** -0.5, 0.1875, ((0, 4),)),
        "head_gain": jnp.clip(1.0 + 0.18 * jax.random.normal(splits[9], (VALUE_DIM,), jnp.float32), 0.099609375, 1.8984375).astype(jnp.bfloat16),
        "w_output": scatter_about(splits[10], (HEADS * VALUE_DIM, D), (HEADS * VALUE_DIM // 2) ** -0.5, 0.1875, ((0, 4),)),
        "mlp_gain": jnp.clip(1.0 + 0.18 * jax.random.normal(splits[11], (D,), jnp.float32), 0.099609375, 1.8984375).astype(jnp.bfloat16),
        "w_gateup": scatter_about(splits[12], (D, 2 * FF), D ** -0.5, 0.1875, ((0, 4),)),
        "w_down": scatter_about(splits[13], (FF, D), (FF // 2) ** -0.5, 0.15625, ((0, 4),)),
        "cotangent": scatter_about(splits[14], (SEQUENCES, LENGTH, D), 1.0, 6.0, ((0, 4), (1, 32))),
    }


epsilon = 1e-06
precise = lax.Precision.HIGHEST

@jax.custom_vjp
def low(v):
    return lax.optimization_barrier(v.astype(jnp.bfloat16)).astype(jnp.float32)

@jax.custom_vjp
def low_back(v):
    return v

def low_keep(v):
    return (low(v), None)

def low_pass(kept, grad):
    return (grad,)

def back_keep(v):
    return (v, None)

def back_low(kept, grad):
    return (low(grad),)
low.defvjp(low_keep, low_pass)
low_back.defvjp(back_keep, back_low)

def product(left, right):
    return jnp.einsum('btd,df->btf', left, right, precision=precise)

def norm_apply(values_in, gain):
    return values_in * lax.rsqrt(lax.optimization_barrier(jnp.mean(values_in * values_in, axis=-1, keepdims=True)) + epsilon) * gain

def swiglu(gateup):
    return jax.nn.silu(gateup[..., :FF]) * gateup[..., FF:]

def gate_heads(outputs, outgate, head_gain):
    normed = outputs * lax.rsqrt(lax.optimization_barrier(jnp.mean(outputs * outputs, axis=-1, keepdims=True)) + epsilon) * head_gain
    return normed.reshape(outgate.shape) * jax.nn.silu(outgate)

def prepare(extended, conv_weight, rate_logits, decay_scale, decay_bias):
    length = extended.shape[1] - (CONV - 1)
    count_seqs = extended.shape[0]
    mixed_conv = sum((conv_weight[lagged] * extended[:, lagged:lagged + length] for lagged in range(CONV)))
    active = jax.nn.silu(mixed_conv)
    keydim = HEADS * KEY_DIM
    queries = active[..., :keydim].reshape(count_seqs, length, HEADS, KEY_DIM)
    keys_in = active[..., keydim:2 * keydim].reshape(count_seqs, length, HEADS, KEY_DIM)
    values = active[..., 2 * keydim:].reshape(count_seqs, length, HEADS, VALUE_DIM)
    queries = queries * lax.rsqrt(lax.optimization_barrier(jnp.sum(queries * queries, axis=-1, keepdims=True)) + epsilon) * KEY_DIM ** (-0.5)
    keys_in = keys_in * lax.rsqrt(lax.optimization_barrier(jnp.sum(keys_in * keys_in, axis=-1, keepdims=True)) + epsilon)
    beta_rates = jax.nn.sigmoid(rate_logits[..., :HEADS])
    decays = -jnp.exp(decay_scale) * jax.nn.softplus(rate_logits[..., HEADS:] + decay_bias)
    return (queries, keys_in, values, beta_rates, decays)

def span_update(state, pieces):
    queries, keys_in, values, beta_rates, decays = pieces
    block_len = queries.shape[2]
    cumlog = jnp.cumsum(decays, axis=2)
    log_gaps = cumlog[..., :, None] - cumlog[..., None, :]
    rows_at = lax.broadcasted_iota(jnp.int32, (block_len, block_len), 0)
    cols_at = lax.broadcasted_iota(jnp.int32, (block_len, block_len), 1)
    strict = cols_at < rows_at
    inclusive = cols_at <= rows_at
    strict_decay = jnp.where(strict, jnp.exp(jnp.where(strict, log_gaps, 0.0)), 0.0)
    incl_decay = jnp.where(inclusive, jnp.exp(jnp.where(inclusive, log_gaps, 0.0)), 0.0)
    key_key = jnp.einsum('bhid,bhjd->bhij', keys_in, keys_in, precision=precise)
    system = jnp.eye(block_len, dtype=jnp.float32) + beta_rates[..., :, None] * strict_decay * key_key
    growth = jnp.exp(cumlog)
    from_state = jnp.einsum('bhid,bhrd->bhir', keys_in, state, precision=precise)
    right_side = beta_rates[..., None] * (values - growth[..., None] * from_state)
    updates = lax.linalg.triangular_solve(system, right_side, left_side=True, lower=True, unit_diagonal=True)
    query_key = jnp.einsum('bhid,bhjd->bhij', queries, keys_in, precision=precise) * incl_decay
    outputs = growth[..., None] * jnp.einsum('bhid,bhrd->bhir', queries, state, precision=precise)
    outputs = outputs + jnp.einsum('bhij,bhjr->bhir', query_key, updates, precision=precise)
    to_end = jnp.exp(cumlog[..., -1:] - cumlog)
    new_state = jnp.exp(cumlog[..., -1])[..., None, None] * state
    new_state = new_state + jnp.einsum('bhir,bhid->bhrd', updates, to_end[..., None] * keys_in, precision=precise)
    return (new_state, outputs)

def to_blocks(values_in):
    count_seqs, length = (values_in.shape[0], values_in.shape[1])
    shaped = values_in.reshape((count_seqs, length // SPAN, SPAN) + values_in.shape[2:])
    return jnp.moveaxis(jnp.moveaxis(shaped, 1, 0), 3, 2)

def from_blocks(blocked):
    moved = jnp.moveaxis(jnp.moveaxis(blocked, 2, 3), 0, 1)
    return moved.reshape((moved.shape[0], moved.shape[1] * moved.shape[2]) + moved.shape[3:])

def run_segment(state, queries, keys_in, values, beta_rates, decays):
    pieces = (to_blocks(queries), to_blocks(keys_in), to_blocks(values), to_blocks(beta_rates), to_blocks(decays))
    final_state, outputs = lax.scan(jax.checkpoint(span_update), state, pieces)
    return (final_state, from_blocks(outputs))

def layer(inputs_f, params):
    gain_one, mixer_w, conv_w, rates_w, scale_w, bias_w, outgate_w, head_w, output_w, gain_two, gateup_w, down_w = params
    hidden_one = low(norm_apply(inputs_f, gain_one))
    mixed_in = low_back(low(product(hidden_one, mixer_w)))
    extended = jnp.pad(mixed_in, ((0, 0), (CONV - 1, 0), (0, 0)))
    rate_logits = low_back(product(hidden_one, rates_w))
    queries, keys_in, values, beta_rates, decays = prepare(extended, conv_w, rate_logits, scale_w, bias_w)
    state_start = jnp.zeros((inputs_f.shape[0], HEADS, VALUE_DIM, KEY_DIM), jnp.float32)
    final_state, outputs = run_segment(state_start, queries, keys_in, values, beta_rates, decays)
    outgate = low_back(product(hidden_one, outgate_w))
    gated_out = low(gate_heads(outputs, outgate, head_w))
    middle = inputs_f + low_back(product(gated_out, output_w))
    hidden_two = low(norm_apply(middle, gain_two))
    gateup = low_back(product(hidden_two, gateup_w))
    activated = low(swiglu(gateup))
    return middle + low_back(product(activated, down_w))

def reference(block_input, seq_lengths, in_gain, w_mixer, conv_weight, w_rates, decay_scale, decay_bias, w_outgate, head_gain, w_output, mlp_gain, w_gateup, w_down, cotangent):
    weights = tuple((member.astype(jnp.float32) for member in (in_gain, w_mixer, conv_weight, w_rates, decay_scale, decay_bias, w_outgate, head_gain, w_output, mlp_gain, w_gateup, w_down)))
    positions = jnp.arange(LENGTH, dtype=jnp.int32)

    def one_sequence(totals, pieces):
        inputs_one, length_one, cot_one = pieces
        valid_mask = (positions < length_one).astype(jnp.float32)[None, :, None]

        def forward(inputs_f, params):
            return layer(inputs_f, params) * valid_mask
        result, pullback = jax.vjp(forward, inputs_one.astype(jnp.float32)[None], weights)
        input_part, weight_parts = pullback(cot_one.astype(jnp.float32)[None])
        totals = tuple((running + added for running, added in zip(totals, weight_parts)))
        return (totals, (result[0].astype(jnp.bfloat16), input_part[0]))
    empty_grads = tuple((jnp.zeros_like(member) for member in weights))
    totals, stacked = lax.scan(one_sequence, empty_grads, (block_input, seq_lengths, cotangent))
    return (stacked[0], stacked[1], totals[0], totals[1], totals[2], totals[3], totals[4], totals[5], totals[6], totals[7], totals[8], totals[9], totals[10], totals[11])
```

```python
import jax
import jax.numpy as jnp
from jax import lax
from jax.sharding import PartitionSpec as P

HEADS = 8
KEY_DIM = 128
HALF = 128
VALUE_DIM = 256
FF = 2816
CONV = 4
CHUNK = 128

epsilon = 1e-06
precise = lax.Precision.HIGHEST
f32 = jnp.float32
bf16 = jnp.bfloat16

CHIPS = [[chip * 2 + core for chip in range(16)] for core in range(2)]
OTHER_CORE = [(place, place ^ 1) for place in range(32)]
OTHER_SEQ = [(place, place ^ 16) for place in range(32)]


def dot(left, right, dims, precision=None):
    return lax.dot_general(left, right, (dims, ((), ())), precision=precision, preferred_element_type=f32)


def mm(left, right):
    return dot(left, right, ((1,), (0,)))


def mm_t(left, right):
    return dot(left, right, ((1,), (1,)))


def t_mm(left, right):
    return dot(left, right, ((0,), (0,)))


def other_core(value):
    return lax.ppermute(value, "ctx", OTHER_CORE)


def other_seq(value):
    return lax.ppermute(value, "ctx", OTHER_SEQ)


def along_grp(value, steps):
    return lax.ppermute(value, "grp", [(at, (at + steps) % 4) for at in range(4)])


def from_grp(value):
    return [value] + [along_grp(value, steps) for steps in (1, 2, 3)]


def in_grp_order(pieces, place):
    turned = [pieces[0], pieces[3], pieces[2], pieces[1]]
    doubled = jnp.stack(turned + turned[:3])
    return lax.dynamic_slice_in_dim(doubled, (4 - place) % 4, 4, axis=0)


def over_chips(value):
    return lax.all_to_all(value, "ctx", 0, 0, axis_index_groups=CHIPS)


def both_cores(mine, core, axis):
    theirs = other_core(mine)
    low = jnp.where(core == 0, mine, theirs)
    high = jnp.where(core == 0, theirs, mine)
    return jnp.stack([low, high], axis=axis)


def to_units(tokens, core):
    received = over_chips(jnp.repeat(tokens, 8, axis=0))
    return both_cores(received, core, 1).reshape(2048, tokens.shape[-1])


def sum_over_units(partial, core):
    split = partial.reshape(16, 2, 64, partial.shape[-1])
    keep = jnp.where(core == 0, split[:, 0], split[:, 1])
    give = jnp.where(core == 0, split[:, 1], split[:, 0]).astype(bf16)
    summed = (keep + other_core(give).astype(f32)).astype(bf16)
    received = over_chips(summed).astype(f32)
    return received.reshape(2, 8, 64, partial.shape[-1]).sum(axis=1)


def prepare(extended, taps):
    length = extended.shape[0] - (CONV - 1)
    mixed_conv = sum(taps[lag] * extended[lag : lag + length] for lag in range(CONV))
    active = jax.nn.silu(mixed_conv)
    queries, keys, values = active[:, :128], active[:, 128:256], active[:, 256:]
    queries = queries * lax.rsqrt(jnp.sum(queries * queries, axis=-1, keepdims=True) + epsilon) * KEY_DIM ** (-0.5)
    keys = keys * lax.rsqrt(jnp.sum(keys * keys, axis=-1, keepdims=True) + epsilon)
    return queries, keys, values


def ein(spec, *args):
    return jnp.einsum(spec, *args, precision=precise)


def inverse_unit_lower(lower):
    size = lower.shape[-1]
    rows = lax.broadcasted_iota(jnp.int32, (size, size), 0)
    cols = lax.broadcasted_iota(jnp.int32, (size, size), 1)
    result = jnp.where(rows == cols, 1.0, 0.0) - jnp.where((rows // 2 == cols // 2), lower, 0.0)
    block = 2
    while block < size:
        mask = (rows // (2 * block) == cols // (2 * block)) & (rows // block != cols // block)
        part = jnp.where(mask, lower, 0.0)
        result = result - ein("nij,njk->nik", result, ein("nij,njk->nik", part, result))
        block *= 2
    return result


def chunk_parts(queries, keys, values, beta, glog):
    total = jnp.cumsum(glog, axis=1)
    rows = lax.broadcasted_iota(jnp.int32, (CHUNK, CHUNK), 0)
    cols = lax.broadcasted_iota(jnp.int32, (CHUNK, CHUNK), 1)
    gaps = total[:, :, None] - total[:, None, :]
    decay = jnp.where(cols <= rows, jnp.exp(jnp.where(cols <= rows, gaps, 0.0)), 0.0)
    lower = jnp.where(cols < rows, decay, 0.0) * ein("nid,njd->nij", keys, keys) * beta[:, :, None]
    inverse = inverse_unit_lower(lower)
    growth = jnp.exp(total)[:, :, None]
    to_end = jnp.exp(total[:, -1:] - total)[:, :, None]
    ending = jnp.exp(total[:, -1])[:, None, None]
    keys_grown = beta[:, :, None] * growth * keys
    from_state = ein("nij,njd->nid", inverse, keys_grown)
    local = ein("nij,njd->nid", inverse, beta[:, :, None] * values)
    scores = ein("nid,njd->nij", queries, keys) * decay
    keys_end = to_end * keys
    transfer = ending * jnp.eye(KEY_DIM, dtype=f32) - ein("nik,nid->nkd", keys_end, from_state)
    added = ein("nik,nir->nkr", keys_end, local)
    probe = growth * queries - ein("nij,njd->nid", scores, from_state)
    return dict(
        decay=decay, inverse=inverse, growth=growth, to_end=to_end, ending=ending, keys_grown=keys_grown,
        from_state=from_state, local=local, scores=scores, keys_end=keys_end, transfer=transfer, added=added,
        probe=probe,
    )


def delta_forward(queries, keys, values, beta, glog):
    parts = chunk_parts(queries, keys, values, beta, glog)

    def step(state, piece):
        transfer, added = piece
        return jnp.matmul(transfer, state, precision=precise) + added, state

    _, states = lax.scan(step, jnp.zeros((KEY_DIM, HALF), f32), (parts["transfer"], parts["added"]))
    updates = parts["local"] - ein("nid,ndr->nir", parts["from_state"], states)
    outputs = parts["growth"] * ein("nid,ndr->nir", queries, states) + ein("nij,njr->nir", parts["scores"], updates)
    return outputs, parts, states, updates


def delta_backward(queries, keys, values, beta, parts, states, updates, grads):
    local = ein("nid,nir->ndr", parts["probe"], grads)

    def step(after, piece):
        transfer, added = piece
        return jnp.matmul(transfer.T, after, precision=precise) + added, after

    _, afters = lax.scan(step, jnp.zeros((KEY_DIM, HALF), f32), (parts["transfer"], local), reverse=True)
    rows = lax.broadcasted_iota(jnp.int32, (CHUNK, CHUNK), 0)
    cols = lax.broadcasted_iota(jnp.int32, (CHUNK, CHUNK), 1)
    d_updates = ein("nij,nir->njr", parts["scores"], grads) + ein("nid,ndr->nir", parts["keys_end"], afters)
    right = ein("nij,nir->njr", parts["inverse"], d_updates)
    d_scores = ein("nir,njr->nij", grads, updates) * parts["decay"]
    d_lower = jnp.where(cols < rows, -ein("nir,njr->nij", right, updates) * parts["decay"], 0.0)
    bcol = beta[:, :, None]
    q_state = parts["growth"] * ein("nir,ndr->nid", grads, states)
    q_keys = ein("nij,njd->nid", d_scores, keys)
    k_queries = ein("nij,nid->njd", d_scores, queries)
    k_rows = ein("nij,njd->nid", d_lower, keys)
    k_cols = ein("nij,nid->njd", d_lower, bcol * keys)
    k_state = parts["growth"] * ein("nir,ndr->nid", right, states)
    k_end = parts["to_end"] * ein("nir,ndr->nid", updates, afters)
    d_queries = q_state + q_keys
    d_keys = k_queries + bcol * k_rows + k_cols + k_end - bcol * k_state
    d_values = bcol * right
    k_sum = lambda value: jnp.sum(keys * value, axis=-1)
    d_beta = k_sum(k_rows) - k_sum(k_state) + jnp.sum(right * values, axis=-1)
    ends = k_sum(k_end)
    d_total = (
        jnp.sum(queries * d_queries, axis=-1)
        - k_sum(k_queries)
        + beta * k_sum(k_rows)
        - k_sum(k_cols)
        - beta * k_sum(k_state)
        - ends
    )
    d_last = jnp.sum(ends, axis=1) + parts["ending"][:, 0, 0] * jnp.sum(states * afters, axis=(1, 2))
    d_total = d_total.at[:, -1].add(d_last)
    d_glog = jnp.flip(jnp.cumsum(jnp.flip(d_total, 1), axis=1), 1)
    return d_queries, d_keys, d_values, d_beta, d_glog


def body(
    block_input,
    seq_lengths,
    in_gain,
    w_mixer,
    conv_weight,
    w_rates,
    decay_scale,
    decay_bias,
    w_outgate,
    head_gain,
    w_output,
    mlp_gain,
    w_gateup,
    w_down,
    cotangent,
):
    place = lax.axis_index("ctx")
    grp = lax.axis_index("grp")
    core = place % 2
    head = (place % 16) // 2
    seq = place // 16

    small = jnp.concatenate(
        [
            w_rates.reshape(-1),
            conv_weight.reshape(-1),
            in_gain,
            mlp_gain,
            head_gain,
            decay_scale,
            decay_bias,
            jnp.zeros((60,), bf16),
        ]
    ).reshape(-1, 128)
    small = in_grp_order(from_grp(small), grp).reshape(4, -1)
    rates_full = small[:, :4096].reshape(1024, 16)
    conv_full = small[:, 4096:8192].reshape(4, 4, 1024).transpose(1, 0, 2).reshape(4, 4096).astype(f32)
    gain_one = small[:, 8192:8448].reshape(1024).astype(f32)
    gain_two = small[:, 8448:8704].reshape(1024).astype(f32)
    head_full = small[:, 8704:8768].reshape(256).astype(f32)
    scale_full = small[:, 8768:8770].reshape(8).astype(f32)
    bias_full = small[:, 8770:8772].reshape(8).astype(f32)

    def unit_columns(value, width=128):
        q_part = lax.dynamic_slice_in_dim(value, head * 128, 128, axis=1)
        k_part = lax.dynamic_slice_in_dim(value, 1024 + head * 128, 128, axis=1)
        v_part = lax.dynamic_slice_in_dim(value, 2048 + place % 16 * 128, 128, axis=1)
        return jnp.concatenate([q_part, k_part, v_part], axis=1)

    outgate_part = lax.dynamic_slice_in_dim(w_outgate, place % 16 * 128, 128, axis=1)
    unit_part = jnp.concatenate([unit_columns(w_mixer), outgate_part], axis=1)
    w_unit = in_grp_order(from_grp(unit_part), grp).reshape(1024, 512)
    w_unit_rates = jnp.stack(
        [
            lax.dynamic_index_in_dim(rates_full, head, 1, False),
            lax.dynamic_index_in_dim(rates_full, 8 + head, 1, False),
        ],
        axis=1,
    )
    taps = unit_columns(conv_full)
    scale = lax.dynamic_index_in_dim(scale_full, head, 0, False)
    bias = lax.dynamic_index_in_dim(bias_full, head, 0, False)
    head_half = lax.dynamic_slice_in_dim(head_full, core * 128, 128, axis=0)

    def ff_columns(owner):
        at = owner * 704 + core * 352
        gate = lax.dynamic_slice_in_dim(w_gateup, at, 352, axis=1)
        up = lax.dynamic_slice_in_dim(w_gateup, FF + at, 352, axis=1)
        return jnp.concatenate([gate, up], axis=1)

    gateup_pieces = [ff_columns(grp)] + [along_grp(ff_columns((grp + steps) % 4), steps) for steps in (1, 2, 3)]
    w_gu = in_grp_order(gateup_pieces, grp).reshape(1024, 704)
    w_dn = lax.dynamic_slice_in_dim(w_down, core * 352, 352, axis=0)
    output_full = lax.all_gather(w_output, "grp", axis=0, tiled=True)
    output_unit = lax.dynamic_slice_in_dim(output_full, place % 16 * 128, 128, axis=0)

    positions = place * 64 + lax.broadcasted_iota(jnp.int32, (2, 64), 1)
    valid = (positions < seq_lengths[:, None]).astype(f32)[..., None]
    inputs_f = block_input.astype(f32)
    inputs_rows = inputs_f.reshape(128, 1024)
    r_one = lax.rsqrt(jnp.mean(inputs_rows * inputs_rows, axis=-1, keepdims=True) + epsilon)
    dy = (cotangent.astype(f32) * valid).reshape(128, 1024)
    dy_low = dy.astype(bf16)

    x_unit = to_units(block_input, core).astype(f32)
    r_unit = lax.rsqrt(jnp.mean(x_unit * x_unit, axis=-1, keepdims=True) + epsilon)
    hidden_one = (x_unit * r_unit * gain_one).astype(bf16)
    projected = mm(hidden_one, w_unit)
    mixed_in = projected[:, :384].astype(bf16)
    outgate = projected[:, 384:]
    rate_logits = mm(hidden_one, w_unit_rates)
    extended = jnp.concatenate([jnp.zeros((3, 384), bf16), mixed_in], axis=0).astype(f32)
    (queries, keys, values), prepare_back = jax.vjp(prepare, extended, taps)
    beta = jax.nn.sigmoid(rate_logits[:, 0])
    decay_in = rate_logits[:, 1] + bias
    glog = -jnp.exp(scale) * jax.nn.softplus(decay_in)
    chunked = lambda value: value.reshape((16, CHUNK) + value.shape[1:])
    queries, keys, values, beta_c, glog_c = map(chunked, (queries, keys, values, beta, glog))
    heads_out, parts, states, updates = delta_forward(queries, keys, values, beta_c, glog_c)
    heads_out = heads_out.reshape(2048, HALF)
    squares = jnp.sum(heads_out * heads_out, axis=-1)
    r_head = lax.rsqrt((squares + other_core(squares)) / VALUE_DIM + epsilon)[:, None]
    normed = heads_out * r_head
    sg = jax.nn.silu(outgate)
    gated = (normed * head_half * sg).astype(bf16)

    gated_tokens = lax.all_to_all(gated.reshape(32, 64, 128), "ctx", 0, 0)
    gated_tokens = gated_tokens.reshape(2, 16, 64, 128).transpose(0, 2, 1, 3).reshape(128, 2048)
    middle = inputs_rows + mm(gated_tokens, output_full)
    r_two = lax.rsqrt(jnp.mean(middle * middle, axis=-1, keepdims=True) + epsilon)
    hidden_two = (middle * r_two * gain_two).astype(bf16)

    def to_wide(tokens):
        mine = jnp.concatenate(from_grp(tokens), axis=0)
        return jnp.concatenate([mine, other_core(mine)], axis=0)

    def from_wide(partial):
        mine = partial[:512] + other_core(partial[512:].astype(bf16)).astype(f32)
        low = mine.reshape(4, 128, 1024).astype(bf16)
        total = mine[:128]
        for steps in (1, 2, 3):
            total = total + along_grp(low[steps], -steps).astype(f32)
        return total

    dy_wide = to_wide(dy_low)
    two_wide = to_wide(hidden_two)
    gateup = mm(two_wide, w_gu)
    gate, up = gateup[:, :352], gateup[:, 352:]
    sig = jax.nn.sigmoid(gate)
    silu_gate = gate * sig
    swi = (silu_gate * up).astype(bf16)
    dswi = mm_t(dy_wide, w_dn)
    dgate = dswi * up * (sig * (1.0 + gate * (1.0 - sig)))
    dgateup = jnp.concatenate([dgate, dswi * silu_gate], axis=1).astype(bf16)
    dhidden_two = from_wide(mm_t(dgateup, w_gu))
    scaled = dhidden_two * gain_two
    dmiddle = dy + r_two * scaled - middle * r_two**3 * jnp.mean(scaled * middle, axis=-1, keepdims=True)
    dmix = dmiddle.astype(bf16)
    dmix_unit = to_units(dmix.reshape(2, 64, 1024), core)

    block_out = middle + from_wide(mm(swi, w_dn))
    block_output = (block_out.reshape(2, 64, 1024) * valid).astype(bf16)

    g_gu = t_mm(two_wide, dgateup)
    g_dn = t_mm(dy_wide, swi)
    g_ff = jnp.concatenate([g_gu, g_dn], axis=1).reshape(4, 16, 16, 1056).transpose(1, 0, 2, 3)
    g_ff = lax.psum_scatter(g_ff.reshape(1024, 1056), "ctx", scatter_dimension=0, tiled=True, axis_index_groups=CHIPS)
    g_ff = g_ff.astype(bf16).reshape(4, 16, 1056)
    g_gu_low = g_ff[:, :, :704]
    g_gu_pieces = [lax.dynamic_index_in_dim(g_gu_low, grp, 0, False)] + [
        along_grp(lax.dynamic_index_in_dim(g_gu_low, (grp + steps) % 4, 0, False), steps) for steps in (1, 2, 3)
    ]
    g_gu_mine = in_grp_order(g_gu_pieces, grp)
    ff_payload = jnp.concatenate([g_gu_mine, g_ff[:, :, 704:]], axis=2)
    ff_all = lax.all_gather(ff_payload, "ctx")
    ff_all = ff_all.reshape(16, 2, 4, 16, 1056).astype(f32)
    grad_gateup = ff_all[..., :704].reshape(16, 2, 4, 16, 2, 352).transpose(0, 3, 4, 2, 1, 5).reshape(256, 5632)
    grad_down = ff_all[..., 704:].transpose(1, 4, 2, 0, 3).reshape(704, 1024)
    grad_mlp_gain = jnp.sum(grad_gateup * w_gateup.astype(f32), axis=1) / mlp_gain.astype(f32)

    dgated = mm_t(dmix_unit, output_unit)
    g_output = t_mm(gated, dmix_unit)
    g_head = jnp.sum(dgated * normed * sg, axis=0)
    sig_og = jax.nn.sigmoid(outgate)
    doutgate = (dgated * head_half * normed * (sig_og * (1.0 + outgate * (1.0 - sig_og)))).astype(bf16)
    dnormed = dgated * head_half * sg
    inner = jnp.sum(dnormed * heads_out, axis=-1)
    inner = ((inner + other_core(inner)) / VALUE_DIM)[:, None]
    dheads = r_head * dnormed - heads_out * r_head**3 * inner
    d_queries, d_keys, d_values, d_beta, d_glog = delta_backward(
        queries, keys, values, beta_c, parts, states, updates, chunked(dheads)
    )
    flat = lambda value: value.reshape((2048,) + value.shape[2:])
    d_ext, g_taps = prepare_back((flat(d_queries), flat(d_keys), flat(d_values)))
    d_ext = jnp.concatenate([d_ext[3:], jnp.zeros((0, 384), f32)], axis=0)
    dmixed = d_ext.astype(bf16)
    d_glog, d_beta = flat(d_glog), flat(d_beta)
    d_decay = -d_glog * jnp.exp(scale) * jax.nn.sigmoid(decay_in)
    g_scale = jnp.sum(d_glog * glog)
    g_bias = jnp.sum(d_decay)
    drates = jnp.stack([d_beta * beta * (1.0 - beta), d_decay], axis=1).astype(bf16)
    d_unit = jnp.concatenate([dmixed, doutgate], axis=1)
    dhidden_one = mm_t(d_unit, w_unit) + mm_t(drates, w_unit_rates)
    g_unit = t_mm(hidden_one, d_unit)
    g_rates = t_mm(drates, hidden_one)

    dhidden_one = sum_over_units(dhidden_one, core).reshape(128, 1024)
    scaled = dhidden_one * gain_one
    input_grad = (
        dmiddle + r_one * scaled - inputs_rows * r_one**3 * jnp.mean(scaled * inputs_rows, axis=-1, keepdims=True)
    )

    g_low = g_unit.astype(bf16).reshape(4, 256, 512)
    g_sum = lax.dynamic_index_in_dim(g_unit.reshape(4, 256, 512), grp, 0, False)
    for steps in (1, 2, 3):
        piece = lax.dynamic_index_in_dim(g_low, (grp + steps) % 4, 0, False)
        g_sum = g_sum + along_grp(piece, steps).astype(f32)
    rows = g_sum.reshape(2, 128, 512)
    mine = lax.dynamic_index_in_dim(rows, seq, 0, False)
    given = lax.dynamic_index_in_dim(rows, 1 - seq, 0, False).astype(bf16)
    mine = mine + other_seq(given).astype(f32)
    halves = mine[:, :256].reshape(2, 64, 256)
    qk_mine = lax.dynamic_index_in_dim(halves, core, 0, False)
    qk_given = lax.dynamic_index_in_dim(halves, 1 - core, 0, False).astype(bf16)
    qk_mine = qk_mine + other_core(qk_given).astype(f32)
    unit_payload = jnp.concatenate([qk_mine.reshape(128, 128), mine[:, 256:384], mine[:, 384:]], axis=1).astype(bf16)
    unit_all = lax.all_gather(unit_payload, "ctx").reshape(2, 8, 2, 128, 384).astype(f32)
    qk_all = unit_all[..., :128].reshape(2, 8, 2, 64, 2, 128)
    grad_qk = qk_all.transpose(0, 2, 3, 4, 1, 5).reshape(256, 2048)
    grad_v = unit_all[..., 128:256].transpose(0, 3, 1, 2, 4).reshape(256, 2048)
    grad_outgate = unit_all[..., 256:].transpose(0, 3, 1, 2, 4).reshape(256, 2048)
    grad_mixer = jnp.concatenate([grad_qk, grad_v], axis=1)

    rows = g_output.reshape(2, 64, 1024)
    mine = lax.dynamic_index_in_dim(rows, seq, 0, False)
    given = lax.dynamic_index_in_dim(rows, 1 - seq, 0, False).astype(bf16)
    mine = (mine + other_seq(given).astype(f32)).reshape(4, 16, 1024)
    low = mine.astype(bf16)
    total = lax.dynamic_index_in_dim(mine, grp, 0, False)
    for steps in (1, 2, 3):
        piece = lax.dynamic_index_in_dim(low, (grp + steps) % 4, 0, False)
        total = total + along_grp(piece, steps).astype(f32)
    moves = []
    for at in range(4):
        for s_at in range(2):
            for h_at in range(8):
                for v_at in range(2):
                    source = at * 32 + s_at * 16 + h_at * 2 + v_at
                    target = (h_at // 2) * 32 + s_at * 16 + ((h_at % 2) * 4 + at) * 2 + v_at
                    moves.append((source, target))
    total = lax.ppermute(total.astype(bf16), ("grp", "ctx"), moves)
    output_all = lax.all_gather(total, "ctx").reshape(2, 2, 4, 2, 16, 1024)
    grad_output = output_all.transpose(1, 3, 0, 2, 4, 5).reshape(512, 1024).astype(f32)

    spread = jnp.zeros((4, 4096), f32)
    spread = lax.dynamic_update_slice(spread, g_taps[:, :128], (0, head * 128))
    spread = lax.dynamic_update_slice(spread, g_taps[:, 128:256], (0, 1024 + head * 128))
    spread = lax.dynamic_update_slice(spread, g_taps[:, 256:], (0, 2048 + place % 16 * 128))
    rates_spread = jnp.zeros((2, 8, 1024), f32)
    rates_spread = lax.dynamic_update_slice(rates_spread, g_rates[:, None], (0, head, 0))
    head_spread = lax.dynamic_update_slice(jnp.zeros((256,), f32), g_head, (core * 128,))
    scale_spread = jnp.where(jnp.arange(8) == head, g_scale, 0.0)
    bias_spread = jnp.where(jnp.arange(8) == head, g_bias, 0.0)
    spread, rates_spread, head_spread, scale_spread, bias_spread = lax.psum(
        (spread, rates_spread, head_spread, scale_spread, bias_spread), ("grp", "ctx")
    )
    grad_conv = lax.dynamic_slice_in_dim(spread, grp * 1024, 1024, axis=1)
    grad_rates = lax.dynamic_slice_in_dim(rates_spread.reshape(16, 1024), grp * 256, 256, axis=1).T
    grad_head = lax.dynamic_slice_in_dim(head_spread, grp * 64, 64, axis=0)
    grad_scale = lax.dynamic_slice_in_dim(scale_spread, grp * 2, 2, axis=0)
    grad_bias = lax.dynamic_slice_in_dim(bias_spread, grp * 2, 2, axis=0)
    grad_in_gain = (
        jnp.sum(grad_mixer * w_mixer.astype(f32), axis=1)
        + jnp.sum(grad_outgate * w_outgate.astype(f32), axis=1)
        + jnp.sum(grad_rates * w_rates.astype(f32), axis=1)
    ) / in_gain.astype(f32)

    return (
        block_output,
        input_grad.reshape(2, 64, 1024),
        grad_in_gain,
        grad_mixer,
        grad_conv,
        grad_rates,
        grad_scale,
        grad_bias,
        grad_outgate,
        grad_head,
        grad_output,
        grad_mlp_gain,
        grad_gateup,
        grad_down,
    )


def solution(mesh):
    placed = (
        P("grp", "ctx", None),
        P("grp"),
        P("grp"),
        P("grp", None),
        P(None, "grp"),
        P("grp", None),
        P("grp"),
        P("grp"),
        P("grp", None),
        P("grp"),
        P("grp", None),
        P("grp"),
        P("grp", None),
        P("grp", None),
        P("grp", "ctx", None),
    )
    return jax.shard_map(
        body,
        mesh=mesh,
        in_specs=placed,
        out_specs=(
            P("grp", "ctx", None),
            P("grp", "ctx", None),
            P("grp"),
            P("grp", None),
            P(None, "grp"),
            P("grp", None),
            P("grp"),
            P("grp"),
            P("grp", None),
            P("grp"),
            P("grp", None),
            P("grp"),
            P("grp", None),
            P("grp", None),
        ),
        check_vma=False,
    )
```

```python
import jax
import jax.numpy as jnp
from jax import lax
from jax.experimental import pallas as pl
from jax.experimental.pallas import tpu as pltpu
from jax.sharding import PartitionSpec as P

f32 = jnp.float32
bf16 = jnp.bfloat16
epsilon = 1e-06
CONV = 4
CHUNK = 128
GROUP = 4
ROWS = CHUNK * GROUP

FF = 2816

CHIPS = [[chip * 2 + core for chip in range(16)] for core in range(2)]
OTHER_CORE = [(place, place ^ 1) for place in range(32)]
OTHER_SEQ = [(place, place ^ 16) for place in range(32)]
OUTPUT_MOVES = [
    (at * 32 + s * 16 + h * 2 + v, (h // 2) * 32 + s * 16 + ((h % 2) * 4 + at) * 2 + v)
    for at in range(4)
    for s in range(2)
    for h in range(8)
    for v in range(2)
]

NN = ((1,), (0,))
NT = ((1,), (1,))
TN = ((0,), (0,))


def raw(left, right, dims):
    return lax.dot_general(left, right, (dims, ((), ())), preferred_element_type=f32)


def split(value):
    high = value.astype(bf16)
    return high, (value - high.astype(f32)).astype(bf16)


def split3(value):
    high = value.astype(bf16)
    rest = value - high.astype(f32)
    mid = rest.astype(bf16)
    return high, mid, (rest - mid.astype(f32)).astype(bf16)


def dot3(left, right, dims):
    lefts = jnp.concatenate([left[0], left[0], left[1]], axis=dims[0][0])
    rights = jnp.concatenate([right[0], right[1], right[0]], axis=dims[1][0])
    return raw(lefts, rights, dims)


def stacked(*pairs, axis=0):
    return tuple(jnp.concatenate([pair[part] for pair in pairs], axis=axis) for part in (0, 1))


def square_iota():
    rows = lax.broadcasted_iota(jnp.int32, (CHUNK, CHUNK), 0)
    cols = lax.broadcasted_iota(jnp.int32, (CHUNK, CHUNK), 1)
    return rows, cols


def inverses(lowers, rows, cols):
    results = [
        jnp.where(rows == cols, 1.0, 0.0) - jnp.where((rows >> 1) == (cols >> 1), lower, 0.0) for lower in lowers
    ]
    level = 1
    while (1 << level) < CHUNK:
        mask = ((rows >> (level + 1)) == (cols >> (level + 1))) & ((rows >> level) != (cols >> level))
        held = [split(result) for result in results]
        parts = [split(jnp.where(mask, lower, 0.0)) for lower in lowers]
        inner = [split(dot3(part, pair, NN)) for part, pair in zip(parts, held)]
        results = [result - dot3(pair, part, NN) for result, pair, part in zip(results, held, inner)]
        level += 1
    return results


def silu(value):
    return value * jax.nn.sigmoid(value)


def softplus(value):
    return jnp.maximum(value, 0.0) + jnp.log1p(jnp.exp(-jnp.abs(value)))


def decay_matrix(total, rows, cols):
    across = total.T[2:3, :]
    return jnp.where(cols <= rows, jnp.exp(jnp.minimum(total[:, 2:3] - across, 0.0)), 0.0)


def unit_norms(active):
    q, k = active[:, :128], active[:, 128:256]
    rq = lax.rsqrt(jnp.sum(q * q, axis=-1, keepdims=True) + epsilon)
    rk = lax.rsqrt(jnp.sum(k * k, axis=-1, keepdims=True) + epsilon)
    return q, k, rq, rk


def forward_kernel(
    numbers, mine, theirs, gain, weight, taps,
    hidden_out, mixed_out, gate_out, conv_out, cols_out, inv_out, from_out, upd_out, score_out, move_out, state_out,
    heads_out, square_out,
    state, ext,
):
    step = pl.program_id(0)
    core, bias, scale = numbers[0], numbers[1], numbers[2]

    @pl.when(step == 0)
    def _():
        state[...] = jnp.zeros_like(state)
        ext[0:8, :] = jnp.zeros((8, 384), f32)

    first = core < 0.5
    for at in range(GROUP):
        one, two = mine[at], theirs[at]
        x = jnp.concatenate([jnp.where(first, one, two), jnp.where(first, two, one)], axis=0).astype(f32)
        rate = lax.rsqrt(jnp.mean(x * x, axis=-1, keepdims=True) + epsilon)
        hidden_out[at * CHUNK : (at + 1) * CHUNK, :] = (x * rate * gain[...]).astype(bf16)
    projected = raw(hidden_out[...], weight[...], NN)
    mixed = projected[:, :384].astype(bf16)
    mixed_out[...] = mixed
    gate_out[...] = projected[:, 384:512]
    rates = projected[:, 512:]
    ext[8 : 8 + ROWS, :] = mixed.astype(f32)
    conv = taps[0:1, :] * ext[5 : 5 + ROWS, :]
    for lag in range(1, CONV):
        conv = conv + taps[lag : lag + 1, :] * ext[5 + lag : 5 + lag + ROWS, :]
    ext[0:8, :] = ext[ROWS : ROWS + 8, :]
    conv_out[...] = conv
    lanes = lax.broadcasted_iota(jnp.int32, (ROWS, 128), 1)
    sums_in = jnp.broadcast_to(rates[:, 1:2], (ROWS, 128)) + bias
    glog = -scale * softplus(sums_in)
    cols_all = jnp.where(lanes == 0, jax.nn.sigmoid(rates), jnp.where(lanes == 3, jax.nn.sigmoid(sums_in), glog))
    rows, cols = square_iota()
    tri = jnp.where(cols <= rows, 1.0, 0.0).astype(bf16)
    tri3 = jnp.concatenate([tri, tri, tri], axis=1)
    lane = lax.broadcasted_iota(jnp.int32, (CHUNK, CHUNK), 1)
    lowers, kept = [], []
    for at in range(GROUP):
        here = slice(at * CHUNK, (at + 1) * CHUNK)
        q, k, rq, rk = unit_norms(silu(conv[here, :256]))
        queries, keys = q * (rq * 128**-0.5), k * rk
        values = silu(conv[here, 256:])
        column = cols_all[here]
        running = raw(tri3, jnp.concatenate(split3(column), axis=0), NN)
        column = jnp.where(lane == 2, running, column)
        cols_out[here, :] = column
        decay = decay_matrix(column, rows, cols)
        beta = column[:, 0:1]
        total = column[:, 2:3]
        growth = jnp.exp(total)
        last = total[CHUNK - 1 : CHUNK, :]
        keys_s = split(keys)
        queries_s = split(queries)
        products = dot3(stacked(keys_s, queries_s), keys_s, NT)
        lowers.append(jnp.where(cols < rows, decay, 0.0) * products[:CHUNK] * beta)
        scores = products[CHUNK:] * decay
        score_out[here, :] = scores
        right = split(jnp.concatenate([(beta * growth) * keys, beta * values], axis=1))
        ends = split(jnp.exp(last - total) * keys)
        kept.append((split(scores), right, ends, split(growth * queries), jnp.exp(last)))
    found = inverses(lowers, rows, cols)
    both = []
    for at in range(GROUP):
        here = slice(at * CHUNK, (at + 1) * CHUNK)
        inv_out[here, :] = found[at]
        both.append(dot3(split(found[at]), kept[at][1], NN))
    maps = []
    for at in range(GROUP):
        here = slice(at * CHUNK, (at + 1) * CHUNK)
        from_out[here, :] = both[at][:, :128]
        ended = dot3(kept[at][2], split(both[at]), TN)
        move = jnp.where(rows == cols, kept[at][4], 0.0) - ended[:, :128]
        move_out[here, :] = move
        maps.append((split(move), ended[:, 128:]))
    current = state[...]
    states = []
    for at in range(GROUP):
        here = slice(at * CHUNK, (at + 1) * CHUNK)
        state_out[here, :] = current
        pair = split(current)
        states.append(pair)
        current = dot3(maps[at][0], pair, NN) + maps[at][1]
    state[...] = current
    ones = jnp.ones((8, 256), bf16)
    for at in range(GROUP):
        here = slice(at * CHUNK, (at + 1) * CHUNK)
        product = dot3(stacked(split(both[at][:, :128]), kept[at][3]), states[at], NN)
        updates = both[at][:, 128:] - product[:CHUNK]
        upd_out[here, :] = updates
        heads = product[CHUNK:] + dot3(kept[at][0], split(updates), NN)
        heads_out[here, :] = heads
        squares = raw(ones, jnp.concatenate(split(heads * heads), axis=1), NT)
        square_out[0, at : at + 1, :] = squares[0:1, :]


def forward_call(numbers, mine, theirs, gain, weight, taps):
    steps = 16 // GROUP
    shape = jax.ShapeDtypeStruct
    blocks = lambda width: pl.BlockSpec((ROWS, width), lambda i: (i, 0))
    whole = lambda *dims: pl.BlockSpec(dims, lambda i: (0,) * len(dims))
    square = shape((2048, 128), f32)
    return pl.pallas_call(
        forward_kernel,
        grid=(steps,),
        in_specs=[
            pl.BlockSpec(memory_space=pltpu.SMEM),
            pl.BlockSpec((GROUP, 64, 1024), lambda i: (i, 0, 0)),
            pl.BlockSpec((GROUP, 64, 1024), lambda i: (i, 0, 0)),
            whole(1, 1024),
            whole(1024, 640),
            whole(4, 384),
        ],
        out_specs=[blocks(1024), blocks(384), blocks(128), blocks(384)]
        + [blocks(128)] * 8
        + [pl.BlockSpec((1, GROUP, 128), lambda i: (i, 0, 0))],
        out_shape=[
            shape((2048, 1024), bf16),
            shape((2048, 384), bf16),
            square,
            shape((2048, 384), f32),
        ]
        + [square] * 8
        + [shape((steps, GROUP, 128), f32)],
        scratch_shapes=[pltpu.VMEM((128, 128), f32), pltpu.VMEM((ROWS + 8, 384), f32)],
        compiler_params=pltpu.CompilerParams(
            dimension_semantics=("arbitrary",), vmem_limit_bytes=52 * 1024 * 1024
        ),
        cost_estimate=cost(30),
        name="delta_forward",
    )(numbers, mine, theirs, gain, weight, taps)


def backward_kernel(
    numbers, taps, conv_in, cols_in, inv_in, from_in, upd_in, score_in, move_in, state_in, mixed_in,
    normed_in, heads_in, sq_mine, sq_theirs, in_mine, in_theirs, hidden_in, gate_in, weight,
    keep_out, give_out, unit_out, logits_out, taps_out, sums_out,
    after, ext, d_all,
):
    step = pl.program_id(0)
    scale = numbers[2]

    @pl.when(step == 0)
    def _():
        after[...] = jnp.zeros_like(after)
        ext[ROWS : ROWS + 8, :] = jnp.zeros((8, 384), f32)
        taps_out[...] = jnp.zeros_like(taps_out)
        sums_out[...] = jnp.zeros_like(sums_out)
        unit_out[...] = jnp.zeros_like(unit_out)
        logits_out[...] = jnp.zeros_like(logits_out)

    rows, cols = square_iota()
    strict = cols < rows
    kept, maps = [], []
    for at in range(GROUP):
        here = slice(at * CHUNK, (at + 1) * CHUNK)
        q, k, rq, rk = unit_norms(silu(conv_in[here, :256]))
        queries, keys = q * (rq * 128**-0.5), k * rk
        column = cols_in[here, :]
        total = column[:, 2:3]
        growth = jnp.exp(total)
        last = total[CHUNK - 1 : CHUNK, :]
        rate = head_rates(sq_mine, sq_theirs, at)
        mean = row_to_square((in_mine[0, at : at + 1, :] + in_theirs[0, at : at + 1, :]) / 256.0)
        grads = split(rate * (normed_in[here, :] - heads_in[here, :] * (rate * rate * mean)))
        passed = dot3(split(score_in[here, :]), grads, TN)
        probe = stacked(split(growth * queries), split(-from_in[here, :]))
        added = dot3(probe, stacked(grads, split(passed)), TN)
        maps.append((split(move_in[here, :]), added))
        kept.append((queries, keys, rq, rk, grads, passed, column, growth, last))
    current = after[...]
    afters = [None] * GROUP
    for at in reversed(range(GROUP)):
        pair = split(current)
        afters[at] = (current, pair)
        current = dot3(maps[at][0], pair, TN) + maps[at][1]
    after[...] = current
    tri = jnp.where(cols >= rows, 1.0, 0.0).astype(bf16)
    tri3 = jnp.concatenate([tri, tri, tri], axis=1)
    scale_sum = jnp.zeros((CHUNK, CHUNK), f32)
    bias_sum = jnp.zeros((CHUNK, CHUNK), f32)
    for at in range(GROUP):
        here = slice(at * CHUNK, (at + 1) * CHUNK)
        queries, keys, rq, rk, grads, passed, column, growth, last = kept[at]
        beta = column[:, 0:1]
        total = column[:, 2:3]
        decay = decay_matrix(column, rows, cols)
        to_end = jnp.exp(last - total)
        keys_s = split(keys)
        state = state_in[here, :]
        state_s = split(state)
        later, later_s = afters[at]
        updates = split(upd_in[here, :])
        d_updates = passed + dot3(split(to_end * keys), later_s, NN)
        right = dot3(split(inv_in[here, :]), split(d_updates), TN)
        right_s = split(right)
        pair = stacked(grads, right_s)
        inner = dot3(pair, updates, NT)
        d_scores = split(inner[:CHUNK] * decay)
        d_lower = split(jnp.where(strict, -inner[CHUNK:] * decay, 0.0))
        through = dot3(pair, state_s, NT)
        k_end = to_end * dot3(updates, later_s, NT)
        d_pair = stacked(d_scores, d_lower)
        on_keys = dot3(d_pair, keys_s, NN)
        k_cols = dot3(d_pair, stacked(split(queries), split(beta * keys)), TN) + k_end
        d_queries = growth * through[:CHUNK] + on_keys[:CHUNK]
        k_rows = on_keys[CHUNK:] - growth * through[CHUNK:]
        k_beta = beta * k_rows
        d_keys = k_beta + k_cols
        values_conv = conv_in[here, 256:]
        values = silu(values_conv)
        d_beta = jnp.sum(keys * k_rows + right * values, axis=-1, keepdims=True)
        d_total = jnp.sum(queries * d_queries + keys * (k_beta - k_cols), axis=-1, keepdims=True)
        ends = jnp.sum(keys * k_end, axis=0, keepdims=True)
        ends = ends + jnp.exp(last) * jnp.sum(state * later, axis=0, keepdims=True)
        d_last = jnp.sum(ends, axis=1, keepdims=True)
        spread = jnp.broadcast_to(d_total, (CHUNK, CHUNK))
        d_glog = raw(tri3, jnp.concatenate(split3(spread), axis=0), NN) + d_last
        d_decay = -scale * d_glog * column[:, 3:4]
        scale_sum = scale_sum + d_glog * column
        bias_sum = bias_sum + d_decay
        d_all[here, 512:] = jnp.where(
            cols == 0, d_beta * beta * (1.0 - beta), jnp.where(cols == 1, d_decay, 0.0)
        ).astype(bf16)
        q_hat, k_hat = queries * 128**0.5, keys
        d_q = (rq * 128**-0.5) * (d_queries - q_hat * jnp.sum(q_hat * d_queries, axis=-1, keepdims=True))
        d_k = rk * (d_keys - k_hat * jnp.sum(k_hat * d_keys, axis=-1, keepdims=True))
        d_v = beta * right
        conv = conv_in[here, :]
        sig = jax.nn.sigmoid(conv)
        ext[here, :] = jnp.concatenate([d_q, d_k, d_v], axis=1) * (sig * (1.0 + conv * (1.0 - sig)))
    sums_out[0:1, :] += jnp.sum(scale_sum, axis=0, keepdims=True)
    sums_out[1:2, :] += jnp.sum(bias_sum, axis=0, keepdims=True)
    mixed = mixed_in[...].astype(f32)
    d_mixed = jnp.zeros((ROWS, 384), f32)
    for lag in range(CONV):
        moved = ext[CONV - 1 - lag : CONV - 1 - lag + ROWS, :]
        d_mixed = d_mixed + taps[lag : lag + 1, :] * moved
        taps_out[lag : lag + 1, :] += jnp.sum(mixed * moved, axis=0, keepdims=True)
    d_all[:, :384] = d_mixed.astype(bf16)
    d_all[:, 384:512] = gate_in[...]
    ext[ROWS : ROWS + 8, :] = ext[0:8, :]
    hidden = hidden_in[...]
    unit_out[...] += raw(hidden, d_all[:, :384], TN)
    logits_out[...] += raw(d_all[:, 512:], hidden, TN)[:8]
    first = numbers[0] < 0.5
    for at in range(GROUP):
        product = raw(d_all[at * CHUNK : (at + 1) * CHUNK, :], weight[...], NT)
        low, high = product[:64], product[64:]
        keep_out[at] = jnp.where(first, low, high)
        give_out[at] = jnp.where(first, high, low).astype(bf16)


def backward_call(numbers, taps, *arrays):
    steps = 16 // GROUP
    shape = jax.ShapeDtypeStruct
    blocks = lambda width: pl.BlockSpec((ROWS, width), lambda i: (steps - 1 - i, 0))
    halves = pl.BlockSpec((GROUP, 64, 1024), lambda i: (steps - 1 - i, 0, 0))
    lines = pl.BlockSpec((1, GROUP, 128), lambda i: (steps - 1 - i, 0, 0))
    whole = lambda *dims: pl.BlockSpec(dims, lambda i: (0,) * len(dims))
    return pl.pallas_call(
        backward_kernel,
        grid=(steps,),
        in_specs=[pl.BlockSpec(memory_space=pltpu.SMEM), whole(4, 384), blocks(384)]
        + [blocks(128)] * 7
        + [blocks(384), blocks(128), blocks(128)]
        + [lines] * 4
        + [blocks(1024), blocks(128), whole(1024, 640)],
        out_specs=[halves, halves, whole(1024, 384), whole(8, 1024), whole(8, 384), whole(8, 128)],
        out_shape=[
            shape((16, 64, 1024), f32),
            shape((16, 64, 1024), bf16),
            shape((1024, 384), f32),
            shape((8, 1024), f32),
            shape((8, 384), f32),
            shape((8, 128), f32),
        ],
        scratch_shapes=[
            pltpu.VMEM((128, 128), f32),
            pltpu.VMEM((ROWS + 8, 384), f32),
            pltpu.VMEM((ROWS, 640), bf16),
        ],
        compiler_params=pltpu.CompilerParams(
            dimension_semantics=("arbitrary",), vmem_limit_bytes=52 * 1024 * 1024
        ),
        cost_estimate=cost(36),
        name="delta_backward",
    )(numbers, taps, *arrays)


def row_to_square(row):
    return jnp.broadcast_to(row, (CHUNK, CHUNK)).T


def head_rates(mine, theirs, at):
    squares = mine[0, at : at + 1, :] + theirs[0, at : at + 1, :]
    return row_to_square(lax.rsqrt(squares / 256.0 + epsilon))


def gate_kernel(heads, gate, mine, theirs, gain, out):
    for at in range(GROUP):
        here = slice(at * CHUNK, (at + 1) * CHUNK)
        normed = heads[here, :] * head_rates(mine, theirs, at)
        out[here, :] = (normed * gain[...] * silu(gate[here, :])).astype(bf16)


def specs(*widths):
    found = []
    for width in widths:
        if width == "rows":
            found.append(pl.BlockSpec((1, GROUP, 128), lambda i: (i, 0, 0)))
        elif width == "tokens":
            found.append(pl.BlockSpec((GROUP, 64, 1024), lambda i: (i, 0, 0)))
        elif width == "smem":
            found.append(pl.BlockSpec(memory_space=pltpu.SMEM))
        elif isinstance(width, tuple):
            found.append(pl.BlockSpec(width, lambda i, dims=len(width): (0,) * dims))
        else:
            found.append(pl.BlockSpec((ROWS, width), lambda i: (i, 0)))
    return found


def cost(microseconds):
    return pl.CostEstimate(flops=microseconds * 10**9, bytes_accessed=microseconds * 3 * 10**6, transcendentals=0)


def params():
    return pltpu.CompilerParams(dimension_semantics=("arbitrary",), vmem_limit_bytes=52 * 1024 * 1024)


def gate_call(heads, gate, mine, theirs, gain):
    return pl.pallas_call(
        gate_kernel,
        grid=(16 // GROUP,),
        in_specs=specs(128, 128, "rows", "rows", (1, 128)),
        out_specs=specs(128)[0],
        out_shape=jax.ShapeDtypeStruct((2048, 128), bf16),
        compiler_params=params(),
        cost_estimate=cost(3),
        name="gate",
    )(heads, gate, mine, theirs, gain)


def middle_kernel(numbers, gated, tokens, mine, theirs, gain, middle_out, hidden_out):
    core = numbers[0]
    for at in range(2):
        line = tokens[at].astype(f32)
        for weight, parity in ((mine, core), (theirs, 1 - core)):
            found = [gated[at * 16 + grp * 4 + parity * 2 + half] for grp in range(4) for half in range(2)]
            line = line + raw(jnp.concatenate(found, axis=1), weight[...], NN)
        rows = slice(at * 64, at * 64 + 64)
        middle_out[rows, :] = line
        rate = lax.rsqrt(jnp.mean(line * line, axis=-1, keepdims=True) + epsilon)
        hidden_out[rows, :] = (line * rate * gain[...]).astype(bf16)


def middle_call(places, gated, tokens, mine, theirs, gain):
    shape = jax.ShapeDtypeStruct
    return pl.pallas_call(
        middle_kernel,
        in_specs=[pl.BlockSpec(memory_space=pltpu.SMEM)] + [pl.BlockSpec(memory_space=pltpu.VMEM)] * 5,
        out_shape=[shape((128, 1024), f32), shape((128, 1024), bf16)],
        compiler_params=pltpu.CompilerParams(vmem_limit_bytes=52 * 1024 * 1024),
        cost_estimate=cost(4),
        name="middle",
    )(places, gated, tokens, mine, theirs, gain)


def gate_back_kernel(
    numbers, mine, theirs, weight, heads, gate, sq_mine, sq_theirs, gain, gated, hidden,
    normed_out, gate_out, inner_out, early_out, head_out,
    output_sum, gate_sum,
):
    @pl.when(pl.program_id(0) == 0)
    def _():
        output_sum[...] = jnp.zeros_like(output_sum)
        gate_sum[...] = jnp.zeros_like(gate_sum)
        head_out[...] = jnp.zeros_like(head_out)

    first = numbers[0] < 0.5
    ones = jnp.ones((8, 256), bf16)
    for at in range(GROUP):
        here = slice(at * CHUNK, (at + 1) * CHUNK)
        one, two = mine[at], theirs[at]
        grads = jnp.concatenate([jnp.where(first, one, two), jnp.where(first, two, one)], axis=0)
        d_gated = raw(grads, weight[...], NT)
        output_sum[...] += raw(gated[here, :], grads, TN)
        value = heads[here, :]
        normed = value * head_rates(sq_mine, sq_theirs, at)
        logits = gate[here, :]
        sig = jax.nn.sigmoid(logits)
        active = logits * sig
        head_out[0:1, :] += jnp.sum(d_gated * normed * active, axis=0, keepdims=True)
        gained = d_gated * gain[...]
        gate_out[here, :] = (gained * normed * (sig * (1.0 + logits * (1.0 - sig)))).astype(bf16)
        d_normed = gained * active
        normed_out[here, :] = d_normed
        product = raw(ones, jnp.concatenate(split(d_normed * value), axis=1), NT)
        inner_out[0, at : at + 1, :] = product[0:1, :]
    gate_sum[...] += raw(hidden[...], gate_out[...], TN)

    @pl.when(pl.program_id(0) == 16 // GROUP - 1)
    def _():
        for grp in range(4):
            early_out[grp, :256, :] = gate_sum[grp * 256 : grp * 256 + 256, :]
            for part in range(8):
                block = output_sum[grp * 32 : grp * 32 + 32, part * 128 : part * 128 + 128]
                early_out[grp, 256 + part * 32 : 288 + part * 32, :] = block


def gate_back_call(numbers, mine, theirs, weight, *arrays):
    shape = jax.ShapeDtypeStruct
    return pl.pallas_call(
        gate_back_kernel,
        grid=(16 // GROUP,),
        in_specs=specs(
            "smem", "tokens", "tokens", (128, 1024), 128, 128, "rows", "rows", (1, 128), 128, 1024
        ),
        out_specs=specs(128, 128, "rows", (4, 512, 128), (8, 128)),
        out_shape=[
            shape((2048, 128), f32),
            shape((2048, 128), bf16),
            shape((16 // GROUP, GROUP, 128), f32),
            shape((4, 512, 128), f32),
            shape((8, 128), f32),
        ],
        scratch_shapes=[pltpu.VMEM((128, 1024), f32), pltpu.VMEM((1024, 128), f32)],
        compiler_params=params(),
        cost_estimate=cost(9),
        name="gate_back",
    )(numbers, mine, theirs, weight, *arrays)


def ff_weights_kernel(two, grads, swi, dy, out):
    grp = pl.program_id(0)
    found = raw(two[...], grads[...], TN).astype(bf16)
    for chip in range(16):
        for part in range(6):
            at = pl.multiple_of(grp * 96 + part * 16, 16)
            block = found[chip * 16 : chip * 16 + 16, part * 128 : part * 128 + 128]
            out[chip, pl.ds(at, 16), :] = block
    found = raw(swi[...], dy[...], TN).astype(bf16)
    for chip in range(16):
        for part in range(2):
            at = pl.multiple_of(384 + grp * 64 + part * 32, 32)
            if chip < 11:
                block = found[chip * 32 : chip * 32 + 32, part * 128 : part * 128 + 128]
            else:
                block = jnp.zeros((32, 128), bf16)
            out[chip, pl.ds(at, 32), :] = block


def ff_weights_call(two, grads, swi, dy):
    return pl.pallas_call(
        ff_weights_kernel,
        grid=(4,),
        in_specs=[
            pl.BlockSpec((1024, 256), lambda i: (0, i)),
            pl.BlockSpec((1024, 768), lambda i: (0, 0)),
            pl.BlockSpec((1024, 384), lambda i: (0, 0)),
            pl.BlockSpec((1024, 256), lambda i: (0, i)),
        ],
        out_specs=pl.BlockSpec((16, 640, 128), lambda i: (0, 0, 0)),
        out_shape=jax.ShapeDtypeStruct((16, 640, 128), bf16),
        compiler_params=params(),
        cost_estimate=cost(7),
        name="ff_weights",
    )(two, grads, swi, dy)


def ff_grads_kernel(numbers, mine, theirs, weight, gain, gateup_out, down_out, gain_out):
    step = pl.program_id(0)
    first = numbers[0] < 0.5

    def piece(core, chip, at, size):
        one, two = mine[chip, at : at + size, :], theirs[chip, at : at + size, :]
        return (jnp.where(first, one, two) if core == 0 else jnp.where(first, two, one)).astype(f32)

    for chip in range(4):
        rows = slice(chip * 16, chip * 16 + 16)
        total = jnp.zeros((16, 128), f32)
        for half in range(2):
            found = []
            for grp in range(4):
                for core in range(2):
                    at = (grp * 6 + half * 3) * 16
                    for part in range(3):
                        block = piece(core, chip, at + part * 16, 16)
                        found.append(block if part < 2 else block[:, :96])
            line = jnp.concatenate(found, axis=1)
            gateup_out[rows, half * FF : (half + 1) * FF] = line
            product = line * weight[rows, half * FF : (half + 1) * FF].astype(f32)
            for part in range(FF // 128):
                total = total + product[:, part * 128 : part * 128 + 128]
        total = jnp.sum(total, axis=1, keepdims=True)
        gain_out[rows, :] = jnp.broadcast_to(total, (16, 128)) / gain[rows, :].astype(f32)

        @pl.when(step * 4 + chip < 11)
        def _():
            for core in range(2):
                at = pl.multiple_of(core * 352 + (step * 4 + chip) * 32, 8)
                for part in range(8):
                    down_out[pl.ds(at, 32), part * 128 : part * 128 + 128] = piece(core, chip, 384 + part * 32, 32)


def ff_grads_call(numbers, mine, theirs, weight, gain):
    shape = jax.ShapeDtypeStruct
    return pl.pallas_call(
        ff_grads_kernel,
        grid=(4,),
        in_specs=[
            pl.BlockSpec(memory_space=pltpu.SMEM),
            pl.BlockSpec((4, 640, 128), lambda i: (i, 0, 0)),
            pl.BlockSpec((4, 640, 128), lambda i: (i, 0, 0)),
            pl.BlockSpec((64, 2 * FF), lambda i: (i, 0)),
            pl.BlockSpec((64, 128), lambda i: (i, 0)),
        ],
        out_specs=[
            pl.BlockSpec((64, 2 * FF), lambda i: (i, 0)),
            pl.BlockSpec((704, 1024), lambda i: (0, 0)),
            pl.BlockSpec((64, 128), lambda i: (i, 0)),
        ],
        out_shape=[shape((256, 2 * FF), f32), shape((704, 1024), f32), shape((256, 128), f32)],
        compiler_params=params(),
        cost_estimate=cost(8),
        name="ff_grads",
    )(numbers, mine, theirs, weight, gain)


def out_grads_kernel(numbers, mine, theirs, weight, gate_out, output_out, sum_out):
    first = numbers[0] < 0.5
    for chip in range(16):
        seq, head = chip // 8, chip % 8
        one, two = mine[chip], theirs[chip]
        for core in range(2):
            piece = (jnp.where(first, one, two) if core == 0 else jnp.where(first, two, one)).astype(f32)
            to = head * 256 + core * 128
            gate_out[seq * 128 : seq * 128 + 128, to : to + 128] = piece[:128]
            at = head // 4 * 256 + core * 128 + head % 4 * 32 + seq * 16
            for part in range(8):
                block = piece[128 + part * 16 : 144 + part * 16]
                output_out[at : at + 16, part * 128 : part * 128 + 128] = block
    for rows in (slice(0, 128), slice(128, 256)):
        total = jnp.sum(gate_out[rows, :] * weight[rows, :].astype(f32), axis=1, keepdims=True)
        sum_out[rows, :] = jnp.broadcast_to(total, (128, 128))


def out_grads_call(numbers, mine, theirs, weight):
    shape = jax.ShapeDtypeStruct
    return pl.pallas_call(
        out_grads_kernel,
        grid=(1,),
        in_specs=[
            pl.BlockSpec(memory_space=pltpu.SMEM),
            pl.BlockSpec((16, 256, 128), lambda i: (0, 0, 0)),
            pl.BlockSpec((16, 256, 128), lambda i: (0, 0, 0)),
            pl.BlockSpec((256, 2048), lambda i: (0, 0)),
        ],
        out_specs=[
            pl.BlockSpec((256, 2048), lambda i: (0, 0)),
            pl.BlockSpec((512, 1024), lambda i: (0, 0)),
            pl.BlockSpec((256, 128), lambda i: (0, 0)),
        ],
        out_shape=[shape((256, 2048), f32), shape((512, 1024), f32), shape((256, 128), f32)],
        compiler_params=params(),
        cost_estimate=cost(4),
        name="out_grads",
    )(numbers, mine, theirs, weight)


def mixer_grads_kernel(numbers, mine, theirs, weight, mixer_out, sum_out):
    first = numbers[0] < 0.5
    for head in range(8):
        one, two = mine[head], theirs[head]
        for core in range(2):
            piece = jnp.where(first, one, two) if core == 0 else jnp.where(first, two, one)
            piece = piece.astype(f32)
            rows = slice(core * 64, core * 64 + 64)
            mixer_out[rows, head * 128 : head * 128 + 128] = piece[:64]
            mixer_out[rows, 1024 + head * 128 : 1152 + head * 128] = piece[64:128]
            to = 2048 + head * 256 + core * 128
            mixer_out[:, to : to + 128] = piece[128:256]
    total = jnp.sum(mixer_out[...] * weight[...].astype(f32), axis=1, keepdims=True)
    sum_out[...] = jnp.broadcast_to(total, (128, 128))


def mixer_grads_call(numbers, mine, theirs, weight):
    shape = jax.ShapeDtypeStruct
    return pl.pallas_call(
        mixer_grads_kernel,
        grid=(2,),
        in_specs=[
            pl.BlockSpec(memory_space=pltpu.SMEM),
            pl.BlockSpec((8, 256, 128), lambda i: (i, 0, 0)),
            pl.BlockSpec((8, 256, 128), lambda i: (i, 0, 0)),
            pl.BlockSpec((128, 4096), lambda i: (i, 0)),
        ],
        out_specs=[
            pl.BlockSpec((128, 4096), lambda i: (i, 0)),
            pl.BlockSpec((128, 128), lambda i: (i, 0)),
        ],
        out_shape=[shape((256, 4096), f32), shape((256, 128), f32)],
        compiler_params=params(),
        cost_estimate=cost(4),
        name="mixer_grads",
    )(numbers, mine, theirs, weight)


def mm(left, right):
    return raw(left, right, NN)


def mm_t(left, right):
    return raw(left, right, NT)


def t_mm(left, right):
    return raw(left, right, TN)


def other_core(value):
    return lax.ppermute(value, "ctx", OTHER_CORE)


def other_seq(value):
    return lax.ppermute(value, "ctx", OTHER_SEQ)


def along_grp(value, steps):
    return lax.ppermute(value, "grp", [(at, (at + steps) % 4) for at in range(4)])


def from_grp(value):
    return [value] + [along_grp(value, steps) for steps in (1, 2, 3)]


def in_grp_order(pieces, place):
    turned = [pieces[0], pieces[3], pieces[2], pieces[1]]
    doubled = jnp.stack(turned + turned[:3])
    return lax.dynamic_slice_in_dim(doubled, (4 - place) % 4, 4, axis=0)


def exchange_grp(value, place):
    part = lambda steps: lax.dynamic_index_in_dim(value, (place + steps) % 4, 0, False)
    return [part(0)] + [along_grp(part(steps), steps) for steps in (1, 2, 3)]


def sum_grp(value, place):
    mine, *others = exchange_grp(value.astype(bf16), place)
    total = lax.dynamic_index_in_dim(value, place, 0, False)
    for other in others:
        total = total + other.astype(f32)
    return total


def after(value, *others):
    return lax.optimization_barrier((value,) + others)[0]


def over_chips(value):
    return lax.all_to_all(value, "ctx", 0, 0, axis_index_groups=CHIPS)


def to_units(tokens):
    mine = over_chips(jnp.repeat(tokens, 8, axis=0))
    return mine, other_core(mine)


def wide_columns(value, width):
    return jnp.concatenate([value[:, at * 128 : at * 128 + 128] for at in range(width // 128)], axis=0)


def body(
    block_input,
    seq_lengths,
    in_gain,
    w_mixer,
    conv_weight,
    w_rates,
    decay_scale,
    decay_bias,
    w_outgate,
    head_gain,
    w_output,
    mlp_gain,
    w_gateup,
    w_down,
    cotangent,
):
    place = lax.axis_index("ctx")
    grp = lax.axis_index("grp")
    core = place % 2
    head = (place % 16) // 2
    seq = place // 16
    unit = place % 16

    x_all = jnp.repeat(block_input, 8, axis=0)
    x_mine = over_chips(x_all)
    w_mixer_one, w_output_one, conv_one = lax.optimization_barrier((w_mixer, w_output, conv_weight, x_all))[:3]

    small = jnp.concatenate(
        [
            conv_one.reshape(-1),
            in_gain,
            mlp_gain,
            head_gain,
            decay_scale,
            decay_bias,
            jnp.zeros((60,), bf16),
        ]
    ).reshape(-1, 128)
    small = in_grp_order(from_grp(small), grp).reshape(4, -1)
    conv_full = small[:, :4096].reshape(4, 4, 1024).transpose(1, 0, 2).reshape(4, 4096).astype(f32)
    gain_one = small[:, 4096:4352].reshape(1, 1024).astype(f32)
    gain_two = small[:, 4352:4608].reshape(1, 1024).astype(f32)
    head_full = small[:, 4608:4672].reshape(1, 256).astype(f32)
    scale_full = small[:, 4672:4674].reshape(8).astype(f32)
    bias_full = small[:, 4674:4676].reshape(8).astype(f32)

    def unit_columns(value):
        q_part = lax.dynamic_slice_in_dim(value, head * 128, 128, axis=1)
        k_part = lax.dynamic_slice_in_dim(value, 1024 + head * 128, 128, axis=1)
        v_part = lax.dynamic_slice_in_dim(value, 2048 + unit * 128, 128, axis=1)
        return [q_part, k_part, v_part]

    unit_part = jnp.concatenate(
        unit_columns(w_mixer_one)
        + [
            lax.dynamic_slice_in_dim(w_outgate, unit * 128, 128, axis=1),
            lax.dynamic_slice_in_dim(w_rates, head, 1, axis=1),
            lax.dynamic_slice_in_dim(w_rates, 8 + head, 1, axis=1),
            jnp.zeros((256, 126), bf16),
        ],
        axis=1,
    )
    w_unit = in_grp_order(from_grp(unit_part), grp).reshape(1024, 640)
    taps = jnp.concatenate(unit_columns(conv_full), axis=1)
    scale = lax.dynamic_index_in_dim(scale_full, head, 0, False)
    bias = lax.dynamic_index_in_dim(bias_full, head, 0, False)
    head_half = lax.dynamic_slice_in_dim(head_full, core * 128, 128, axis=1)
    numbers = jnp.stack([core.astype(f32), bias, jnp.exp(scale), jnp.zeros((), f32)])

    def ff_columns(owner):
        at = owner * 704 + core * 352
        gate = lax.dynamic_slice_in_dim(w_gateup, at, 352, axis=1)
        up = lax.dynamic_slice_in_dim(w_gateup, FF + at, 352, axis=1)
        fill = jnp.zeros((256, 32), bf16)
        return jnp.concatenate([gate, fill, up, fill], axis=1)

    gateup_pieces = [ff_columns((grp + steps) % 4) for steps in range(4)]
    w_dn = jnp.concatenate(
        [lax.dynamic_slice_in_dim(w_down, core * 352, 352, axis=0), jnp.zeros((32, 1024), bf16)], axis=0
    )
    output_half = lax.dynamic_slice_in_dim(w_output_one, core * 256, 256, axis=0)
    output_mine = lax.all_gather(output_half, "grp", axis=0, tiled=True)

    positions = place * 64 + lax.broadcasted_iota(jnp.int32, (2, 64), 1)
    valid = (positions < seq_lengths[:, None]).astype(f32)[..., None]
    inputs_rows = block_input.astype(f32).reshape(128, 1024)
    r_one = lax.rsqrt(jnp.mean(inputs_rows * inputs_rows, axis=-1, keepdims=True) + epsilon)
    dy = (cotangent.astype(f32) * valid).reshape(128, 1024)
    dy_low = dy.astype(bf16)

    def to_wide(tokens):
        mine = jnp.concatenate(from_grp(tokens), axis=0)
        return jnp.concatenate([mine, other_core(mine)], axis=0)

    def from_wide(left, right, dims, sent):
        theirs = other_core(raw(left[512:], right, dims).astype(sent))
        mine = raw(left[:512], right, dims) + theirs.astype(f32)
        low = mine.reshape(4, 128, 1024).astype(sent)
        total = mine[:128]
        for steps in (1, 2, 3):
            total = total + along_grp(low[steps], -steps).astype(f32)
        return total

    places = jnp.stack([core, head])
    gateup_pieces, dy_sent, x_mine = lax.optimization_barrier((gateup_pieces, dy_low, x_mine))
    x_theirs = other_core(x_mine)
    dy_pieces = from_grp(dy_sent)
    gateup_pieces = gateup_pieces[:1] + [along_grp(gateup_pieces[steps], steps) for steps in (1, 2, 3)]

    (
        hidden_one, mixed_in, outgate, conv, columns, inverse, from_state, updates, scores, moves, states, heads_out,
        squares,
    ) = forward_call(numbers, x_mine, x_theirs, gain_one, w_unit, taps)
    output_theirs = other_core(output_mine)
    unit_at = head // 2 * 256 + core * 128
    output_unit = jnp.where(
        head % 2 == core,
        lax.dynamic_slice_in_dim(output_mine, unit_at, 128, axis=0),
        lax.dynamic_slice_in_dim(output_theirs, unit_at, 128, axis=0),
    )
    squares_theirs = other_core(squares)
    heads_out, gateup_pieces, dy_pieces = lax.optimization_barrier((heads_out, gateup_pieces, dy_pieces))
    gated = gate_call(heads_out, outgate, squares, squares_theirs, head_half)

    gated_tokens = lax.all_to_all(gated.reshape(32, 64, 128), "ctx", 0, 0)
    middle, hidden_two = middle_call(places, gated_tokens, block_input, output_mine, output_theirs, gain_two)
    r_two = lax.rsqrt(jnp.mean(middle * middle, axis=-1, keepdims=True) + epsilon)
    gateup_pieces, dy_pieces = lax.optimization_barrier((gateup_pieces, dy_pieces, hidden_two))[:2]
    w_gu = in_grp_order(gateup_pieces, grp).reshape(1024, 768)
    dy_wide = jnp.concatenate(dy_pieces, axis=0)
    dy_wide = jnp.concatenate([dy_wide, other_core(dy_wide)], axis=0)
    two_wide = to_wide(hidden_two)
    gateup = mm(two_wide, w_gu)
    gate, up = gateup[:, :384], gateup[:, 384:]
    sig = jax.nn.sigmoid(gate)
    silu_gate = gate * sig
    swi = (silu_gate * up).astype(bf16)
    dswi = mm_t(dy_wide, w_dn)
    dgate = dswi * up * (sig * (1.0 + gate * (1.0 - sig)))
    dgateup = jnp.concatenate([dgate, dswi * silu_gate], axis=1).astype(bf16)
    g_ff = ff_weights_call(two_wide, dgateup, swi, dy_wide)
    dhidden_two = from_wide(dgateup, w_gu, NT, f32)
    scaled = dhidden_two * gain_two
    dmiddle = dy + r_two * scaled - middle * r_two**3 * jnp.mean(scaled * middle, axis=-1, keepdims=True)
    dmix = dmiddle.astype(bf16)
    dmix, g_ff = lax.optimization_barrier((dmix, g_ff))
    dmix_mine, dmix_theirs = to_units(dmix.reshape(2, 64, 1024))

    d_normed, d_outgate, inner, g_early, g_head = gate_back_call(
        numbers, dmix_mine, dmix_theirs, output_unit, heads_out, outgate, squares, squares_theirs, head_half, gated,
        hidden_one,
    )
    inner_theirs = other_core(inner)
    g_ff, g_early, inner, d_normed = lax.optimization_barrier((g_ff, g_early, inner, d_normed))
    g_ff = over_chips(g_ff)
    early_mine, *early_others = exchange_grp(g_early.astype(bf16), grp)
    early_mine = lax.dynamic_index_in_dim(g_early, grp, 0, False)
    keep, give, g_unit, g_rates, g_taps, g_sums = backward_call(
        numbers, taps, conv, columns, inverse, from_state, updates, scores, moves, states, mixed_in,
        d_normed, heads_out, squares, squares_theirs, inner, inner_theirs, hidden_one, d_outgate, w_unit,
    )

    give_theirs = other_core(give)
    d_sent = (keep + give_theirs.astype(f32)).astype(bf16)
    d_tokens = over_chips(d_sent)

    g_rates = g_rates[:2].reshape(2, 4, 2, 128).transpose(1, 0, 2, 3).reshape(4, 4, 128)
    shared = jnp.concatenate(
        [g_taps[:4].reshape(12, 128), g_head[:1], g_sums[:2], jnp.zeros((5, 128), f32)], axis=0
    )
    g_small = jnp.concatenate([jnp.broadcast_to(shared, (4, 20, 128)), g_rates], axis=1)

    g_ff, early_others, give_theirs = lax.optimization_barrier((g_ff, early_others, give_theirs))
    g_ff = g_ff.astype(f32).sum(axis=0).astype(bf16)
    g_gu = in_grp_order(exchange_grp(g_ff[:384].reshape(4, 96, 128), grp), grp).reshape(384, 128)
    g_early = early_mine + sum(other.astype(f32) for other in early_others)
    g_early = jnp.concatenate(
        [g_early[:256].reshape(2, 128, 128), g_early[256:].reshape(8, 2, 16, 128).transpose(1, 0, 2, 3).reshape(2, 128, 128)],
        axis=1,
    )
    early_mine = lax.dynamic_index_in_dim(g_early, seq, 0, False)
    early_given = lax.dynamic_index_in_dim(g_early, 1 - seq, 0, False).astype(bf16)
    early_mine = (early_mine + other_seq(early_given).astype(f32)).astype(bf16)
    early_output = lax.ppermute(early_mine[128:], ("grp", "ctx"), OUTPUT_MOVES)
    early = jnp.concatenate([g_gu, g_ff[384:], early_mine[:128], early_output], axis=0)
    early_mine = lax.all_gather(early, "ctx", axis_index_groups=CHIPS)
    early_theirs = other_core(early_mine)
    grad_gateup, grad_down, mlp_sums = ff_grads_call(
        numbers, early_mine, early_theirs, w_gateup, jnp.broadcast_to(mlp_gain[:, None], (256, 128))
    )
    grad_outgate, grad_output, gate_sums = out_grads_call(
        numbers, early_mine[:, 640:], early_theirs[:, 640:], w_outgate
    )

    swi, g_unit, g_small = lax.optimization_barrier((swi, g_unit, g_small, d_sent))[:3]
    g_small = sum(exchange_grp(g_small, grp))
    g_sum = sum_grp(g_unit.reshape(4, 256, 384), grp).reshape(2, 128, 384)

    dhidden_one = d_tokens.astype(f32)
    dhidden_one = dhidden_one.reshape(2, 8, 64, 1024).sum(axis=1).reshape(128, 1024)
    scaled = dhidden_one * gain_one
    input_grad = (
        dmiddle + r_one * scaled - inputs_rows * r_one**3 * jnp.mean(scaled * inputs_rows, axis=-1, keepdims=True)
    )

    mine = lax.dynamic_index_in_dim(g_sum, seq, 0, False)
    given = lax.dynamic_index_in_dim(g_sum, 1 - seq, 0, False).astype(bf16)
    mine = mine + other_seq(given).astype(f32)
    halves = mine[:, :256].reshape(2, 64, 256)
    qk_mine = lax.dynamic_index_in_dim(halves, core, 0, False)
    qk_given = lax.dynamic_index_in_dim(halves, 1 - core, 0, False).astype(bf16)
    qk_mine = qk_mine + other_core(qk_given).astype(f32)
    late = jnp.concatenate([qk_mine[:, :128], qk_mine[:, 128:], mine[:, 256:]], axis=0).astype(bf16)
    small_high = lax.optimization_barrier(g_small.astype(bf16))
    small_low = (g_small - small_high.astype(f32)).astype(bf16)
    late = jnp.concatenate([late, small_high, small_low], axis=0)
    late, d_tokens = lax.optimization_barrier((late, d_tokens))
    late_mine = over_chips(jnp.broadcast_to(late, (16,) + late.shape))
    late_theirs = other_core(late_mine)
    grad_mixer, mixer_sums = mixer_grads_call(numbers, late_mine, late_theirs, w_mixer)
    small_one = (late_mine[:, 256:280].astype(f32) + late_mine[:, 280:].astype(f32)).reshape(2, 8, 24, 128)
    small_two = (late_theirs[:, 256:280].astype(f32) + late_theirs[:, 280:].astype(f32)).reshape(2, 8, 24, 128)
    small_one, small_two = small_one.sum(axis=0), small_two.sum(axis=0)
    both = small_one + small_two
    g_low = jnp.where(core == 0, small_one, small_two)
    g_high = jnp.where(core == 0, small_two, small_one)
    taps_at = lambda value, at: value[:, :12].reshape(8, 4, 3, 128)[:, :, at].transpose(1, 0, 2).reshape(4, 1024)
    taps_v = jnp.stack([g_low[:, :12], g_high[:, :12]], axis=1).reshape(8, 2, 4, 3, 128)[:, :, :, 2]
    taps_v = taps_v.transpose(2, 0, 1, 3).reshape(4, 2048)
    grad_conv = jnp.concatenate([taps_at(both, 0), taps_at(both, 1), taps_v], axis=1)
    grad_conv = lax.dynamic_slice_in_dim(grad_conv, grp * 1024, 1024, axis=1)
    grad_head = jnp.concatenate([g_low[:, 12].sum(axis=0), g_high[:, 12].sum(axis=0)])
    grad_head = lax.dynamic_slice_in_dim(grad_head, grp * 64, 64, axis=0)
    grad_scale = lax.dynamic_slice_in_dim(both[:, 13, 1], grp * 2, 2, axis=0)
    grad_bias = lax.dynamic_slice_in_dim(both[:, 14, 1], grp * 2, 2, axis=0)
    grad_rates = both[:, 20:].reshape(8, 2, 256).transpose(1, 0, 2).reshape(16, 256).T
    grad_in_gain = (
        mixer_sums[:, 0]
        + gate_sums[:, 0]
        + jnp.sum(grad_rates * w_rates.astype(f32), axis=1)
    ) / in_gain.astype(f32)

    block_out = middle + from_wide(swi, w_dn, NN, bf16)
    block_output = (block_out.reshape(2, 64, 1024) * valid).astype(bf16)

    return (
        block_output,
        input_grad.reshape(2, 64, 1024),
        grad_in_gain,
        grad_mixer,
        grad_conv,
        grad_rates,
        grad_scale,
        grad_bias,
        grad_outgate,
        grad_head,
        grad_output,
        mlp_sums[:, 0],
        grad_gateup,
        grad_down,
    )


def solution(mesh):
    tokens = P("grp", "ctx", None)
    rows = P("grp", None)
    one = P("grp")
    taps = P(None, "grp")
    return jax.shard_map(
        body,
        mesh=mesh,
        in_specs=(tokens, one, one, rows, taps, rows, one, one, rows, one, rows, one, rows, rows, tokens),
        out_specs=(tokens, tokens, one, rows, taps, rows, one, one, rows, one, rows, one, rows, rows),
        check_vma=False,
    )
```

```python
import jax
import jax.numpy as jnp
from jax import lax
from jax.experimental import pallas as pl
from jax.experimental.pallas import tpu as pltpu
from jax.sharding import PartitionSpec as P

f32 = jnp.float32
bf16 = jnp.bfloat16
epsilon = 1e-06
CONV = 4
CHUNK = 128
GROUP = 4
ROWS = CHUNK * GROUP

FF = 2816

CHIPS = [[chip * 2 + core for chip in range(16)] for core in range(2)]
OTHER_CORE = [(place, place ^ 1) for place in range(32)]
OTHER_SEQ = [(place, place ^ 16) for place in range(32)]

NN = ((1,), (0,))
NT = ((1,), (1,))
TN = ((0,), (0,))


def raw(left, right, dims):
    return lax.dot_general(left, right, (dims, ((), ())), preferred_element_type=f32)


def split(value):
    high = value.astype(bf16)
    return high, (value - high.astype(f32)).astype(bf16)


def split3(value):
    high = value.astype(bf16)
    rest = value - high.astype(f32)
    mid = rest.astype(bf16)
    return high, mid, (rest - mid.astype(f32)).astype(bf16)


def dot3(left, right, dims):
    lefts = jnp.concatenate([left[0], left[0], left[1]], axis=dims[0][0])
    rights = jnp.concatenate([right[0], right[1], right[0]], axis=dims[1][0])
    return raw(lefts, rights, dims)


def stacked(*pairs, axis=0):
    return tuple(jnp.concatenate([pair[part] for pair in pairs], axis=axis) for part in (0, 1))


def square_iota():
    rows = lax.broadcasted_iota(jnp.int32, (CHUNK, CHUNK), 0)
    cols = lax.broadcasted_iota(jnp.int32, (CHUNK, CHUNK), 1)
    return rows, cols


def inverses(lowers, rows, cols):
    results = [
        jnp.where(rows == cols, 1.0, 0.0) - jnp.where((rows >> 1) == (cols >> 1), lower, 0.0) for lower in lowers
    ]
    level = 1
    while (1 << level) < CHUNK:
        mask = ((rows >> (level + 1)) == (cols >> (level + 1))) & ((rows >> level) != (cols >> level))
        held = [split(result) for result in results]
        parts = [split(jnp.where(mask, lower, 0.0)) for lower in lowers]
        inner = [split(dot3(part, pair, NN)) for part, pair in zip(parts, held)]
        results = [result - dot3(pair, part, NN) for result, pair, part in zip(results, held, inner)]
        level += 1
    return results


def silu(value):
    return value * jax.nn.sigmoid(value)


def softplus(value):
    return jnp.maximum(value, 0.0) + jnp.log1p(jnp.exp(-jnp.abs(value)))


def decay_matrix(total, rows, cols):
    across = total.T[2:3, :]
    return jnp.where(cols <= rows, jnp.exp(jnp.minimum(total[:, 2:3] - across, 0.0)), 0.0)


def unit_norms(active):
    q, k = active[:, :128], active[:, 128:256]
    rq = lax.rsqrt(jnp.sum(q * q, axis=-1, keepdims=True) + epsilon)
    rk = lax.rsqrt(jnp.sum(k * k, axis=-1, keepdims=True) + epsilon)
    return q, k, rq, rk


def block_of(places, steps):
    return pl.ds(pl.multiple_of(places[2 + steps] * 256, 256), 256)


def forward_kernel(
    numbers, places, mine, theirs, gain, weight_0, weight_1, weight_2, weight_3, taps,
    hidden_out, mixed_out, gate_out, conv_out, cols_out, inv_out, from_out, upd_out, score_out, move_out, state_out,
    heads_out, square_out,
    state, ext, held,
):
    step = pl.program_id(0)
    core, bias, scale = numbers[0], numbers[1], numbers[2]

    @pl.when(step == 0)
    def _():
        state[...] = jnp.zeros_like(state)
        ext[0:8, :] = jnp.zeros((8, 384), f32)
        for steps, weight in enumerate((weight_0, weight_1, weight_2, weight_3)):
            held[block_of(places, steps), :] = weight[...]

    first = core < 0.5
    for at in range(GROUP):
        one, two = mine[at], theirs[at]
        x = jnp.concatenate([jnp.where(first, one, two), jnp.where(first, two, one)], axis=0).astype(f32)
        rate = lax.rsqrt(jnp.mean(x * x, axis=-1, keepdims=True) + epsilon)
        hidden_out[at * CHUNK : (at + 1) * CHUNK, :] = (x * rate * gain[...]).astype(bf16)
    projected = raw(hidden_out[...], held[...], NN)
    mixed = projected[:, :384].astype(bf16)
    mixed_out[...] = mixed
    gate_out[...] = projected[:, 384:512]
    rates = projected[:, 512:]
    ext[8 : 8 + ROWS, :] = mixed.astype(f32)
    conv = taps[0:1, :] * ext[5 : 5 + ROWS, :]
    for lag in range(1, CONV):
        conv = conv + taps[lag : lag + 1, :] * ext[5 + lag : 5 + lag + ROWS, :]
    ext[0:8, :] = ext[ROWS : ROWS + 8, :]
    conv_out[...] = conv
    lanes = lax.broadcasted_iota(jnp.int32, (ROWS, 128), 1)
    sums_in = jnp.broadcast_to(rates[:, 1:2], (ROWS, 128)) + bias
    glog = -scale * softplus(sums_in)
    cols_all = jnp.where(lanes == 0, jax.nn.sigmoid(rates), jnp.where(lanes == 3, jax.nn.sigmoid(sums_in), glog))
    rows, cols = square_iota()
    tri = jnp.where(cols <= rows, 1.0, 0.0).astype(bf16)
    tri3 = jnp.concatenate([tri, tri, tri], axis=1)
    lane = lax.broadcasted_iota(jnp.int32, (CHUNK, CHUNK), 1)
    lowers, kept = [], []
    for at in range(GROUP):
        here = slice(at * CHUNK, (at + 1) * CHUNK)
        q, k, rq, rk = unit_norms(silu(conv[here, :256]))
        queries, keys = q * (rq * 128**-0.5), k * rk
        values = silu(conv[here, 256:])
        column = cols_all[here]
        running = raw(tri3, jnp.concatenate(split3(column), axis=0), NN)
        column = jnp.where(lane == 2, running, column)
        cols_out[here, :] = column
        decay = decay_matrix(column, rows, cols)
        beta = column[:, 0:1]
        total = column[:, 2:3]
        growth = jnp.exp(total)
        last = total[CHUNK - 1 : CHUNK, :]
        keys_s = split(keys)
        queries_s = split(queries)
        products = dot3(stacked(keys_s, queries_s), keys_s, NT)
        lowers.append(jnp.where(cols < rows, decay, 0.0) * products[:CHUNK] * beta)
        scores = products[CHUNK:] * decay
        score_out[here, :] = scores
        right = split(jnp.concatenate([(beta * growth) * keys, beta * values], axis=1))
        ends = split(jnp.exp(last - total) * keys)
        kept.append((split(scores), right, ends, split(growth * queries), jnp.exp(last)))
    found = inverses(lowers, rows, cols)
    both = []
    for at in range(GROUP):
        here = slice(at * CHUNK, (at + 1) * CHUNK)
        inv_out[here, :] = found[at]
        both.append(dot3(split(found[at]), kept[at][1], NN))
    maps = []
    for at in range(GROUP):
        here = slice(at * CHUNK, (at + 1) * CHUNK)
        from_out[here, :] = both[at][:, :128]
        ended = dot3(kept[at][2], split(both[at]), TN)
        move = jnp.where(rows == cols, kept[at][4], 0.0) - ended[:, :128]
        move_out[here, :] = move
        maps.append((split(move), ended[:, 128:]))
    current = state[...]
    states = []
    for at in range(GROUP):
        here = slice(at * CHUNK, (at + 1) * CHUNK)
        state_out[here, :] = current
        pair = split(current)
        states.append(pair)
        current = dot3(maps[at][0], pair, NN) + maps[at][1]
    state[...] = current
    ones = jnp.ones((8, 256), bf16)
    for at in range(GROUP):
        here = slice(at * CHUNK, (at + 1) * CHUNK)
        product = dot3(stacked(split(both[at][:, :128]), kept[at][3]), states[at], NN)
        updates = both[at][:, 128:] - product[:CHUNK]
        upd_out[here, :] = updates
        heads = product[CHUNK:] + dot3(kept[at][0], split(updates), NN)
        heads_out[here, :] = heads
        squares = raw(ones, jnp.concatenate(split(heads * heads), axis=1), NT)
        square_out[0, at : at + 1, :] = squares[0:1, :]


def forward_call(numbers, places, mine, theirs, gain, weights, taps):
    steps = 16 // GROUP
    shape = jax.ShapeDtypeStruct
    blocks = lambda width: pl.BlockSpec((ROWS, width), lambda i: (i, 0))
    whole = lambda *dims: pl.BlockSpec(dims, lambda i: (0,) * len(dims))
    square = shape((2048, 128), f32)
    return pl.pallas_call(
        forward_kernel,
        grid=(steps,),
        in_specs=[
            pl.BlockSpec(memory_space=pltpu.SMEM),
            pl.BlockSpec(memory_space=pltpu.SMEM),
            pl.BlockSpec((GROUP, 64, 1024), lambda i: (i, 0, 0)),
            pl.BlockSpec((GROUP, 64, 1024), lambda i: (i, 0, 0)),
            whole(1, 1024),
        ]
        + [whole(256, 640)] * 4
        + [whole(4, 384)],
        out_specs=[blocks(1024), blocks(384), blocks(128), blocks(384)]
        + [blocks(128)] * 8
        + [pl.BlockSpec((1, GROUP, 128), lambda i: (i, 0, 0))],
        out_shape=[
            shape((2048, 1024), bf16),
            shape((2048, 384), bf16),
            square,
            shape((2048, 384), f32),
        ]
        + [square] * 8
        + [shape((steps, GROUP, 128), f32)],
        scratch_shapes=[
            pltpu.VMEM((128, 128), f32),
            pltpu.VMEM((ROWS + 8, 384), f32),
            pltpu.VMEM((1024, 640), bf16),
        ],
        compiler_params=pltpu.CompilerParams(
            dimension_semantics=("arbitrary",), vmem_limit_bytes=52 * 1024 * 1024
        ),
        cost_estimate=cost(30),
        name="delta_forward",
    )(numbers, places, mine, theirs, gain, *weights, taps)


def backward_kernel(
    numbers, places, taps, conv_in, cols_in, inv_in, from_in, upd_in, score_in, move_in, state_in, mixed_in,
    normed_in, heads_in, sq_mine, sq_theirs, in_mine, in_theirs, hidden_in, gate_in,
    weight_0, weight_1, weight_2, weight_3,
    keep_out, give_out, unit_out, low_out, logits_out, taps_out, sums_out,
    after, ext, d_all, held,
):
    step = pl.program_id(0)
    scale = numbers[2]

    @pl.when(step == 0)
    def _():
        after[...] = jnp.zeros_like(after)
        ext[ROWS : ROWS + 8, :] = jnp.zeros((8, 384), f32)
        taps_out[...] = jnp.zeros_like(taps_out)
        sums_out[...] = jnp.zeros_like(sums_out)
        unit_out[...] = jnp.zeros_like(unit_out)
        logits_out[...] = jnp.zeros_like(logits_out)
        for steps, weight in enumerate((weight_0, weight_1, weight_2, weight_3)):
            held[block_of(places, steps), :] = weight[...]

    rows, cols = square_iota()
    strict = cols < rows
    kept, maps = [], []
    for at in range(GROUP):
        here = slice(at * CHUNK, (at + 1) * CHUNK)
        q, k, rq, rk = unit_norms(silu(conv_in[here, :256]))
        queries, keys = q * (rq * 128**-0.5), k * rk
        column = cols_in[here, :]
        total = column[:, 2:3]
        growth = jnp.exp(total)
        last = total[CHUNK - 1 : CHUNK, :]
        rate = head_rates(sq_mine, sq_theirs, at)
        mean = row_to_square((in_mine[0, at : at + 1, :] + in_theirs[0, at : at + 1, :]) / 256.0)
        grads = split(rate * (normed_in[here, :] - heads_in[here, :] * (rate * rate * mean)))
        passed = dot3(split(score_in[here, :]), grads, TN)
        probe = stacked(split(growth * queries), split(-from_in[here, :]))
        added = dot3(probe, stacked(grads, split(passed)), TN)
        maps.append((split(move_in[here, :]), added))
        kept.append((queries, keys, rq, rk, grads, passed, column, growth, last))
    current = after[...]
    afters = [None] * GROUP
    for at in reversed(range(GROUP)):
        pair = split(current)
        afters[at] = (current, pair)
        current = dot3(maps[at][0], pair, TN) + maps[at][1]
    after[...] = current
    tri = jnp.where(cols >= rows, 1.0, 0.0).astype(bf16)
    tri3 = jnp.concatenate([tri, tri, tri], axis=1)
    scale_sum = jnp.zeros((CHUNK, CHUNK), f32)
    bias_sum = jnp.zeros((CHUNK, CHUNK), f32)
    for at in range(GROUP):
        here = slice(at * CHUNK, (at + 1) * CHUNK)
        queries, keys, rq, rk, grads, passed, column, growth, last = kept[at]
        beta = column[:, 0:1]
        total = column[:, 2:3]
        decay = decay_matrix(column, rows, cols)
        to_end = jnp.exp(last - total)
        keys_s = split(keys)
        state = state_in[here, :]
        state_s = split(state)
        later, later_s = afters[at]
        updates = split(upd_in[here, :])
        d_updates = passed + dot3(split(to_end * keys), later_s, NN)
        right = dot3(split(inv_in[here, :]), split(d_updates), TN)
        right_s = split(right)
        pair = stacked(grads, right_s)
        inner = dot3(pair, updates, NT)
        d_scores = split(inner[:CHUNK] * decay)
        d_lower = split(jnp.where(strict, -inner[CHUNK:] * decay, 0.0))
        through = dot3(pair, state_s, NT)
        k_end = to_end * dot3(updates, later_s, NT)
        d_pair = stacked(d_scores, d_lower)
        on_keys = dot3(d_pair, keys_s, NN)
        k_cols = dot3(d_pair, stacked(split(queries), split(beta * keys)), TN) + k_end
        d_queries = growth * through[:CHUNK] + on_keys[:CHUNK]
        k_rows = on_keys[CHUNK:] - growth * through[CHUNK:]
        k_beta = beta * k_rows
        d_keys = k_beta + k_cols
        values_conv = conv_in[here, 256:]
        values = silu(values_conv)
        d_beta = jnp.sum(keys * k_rows + right * values, axis=-1, keepdims=True)
        d_total = jnp.sum(queries * d_queries + keys * (k_beta - k_cols), axis=-1, keepdims=True)
        ends = jnp.sum(keys * k_end, axis=0, keepdims=True)
        ends = ends + jnp.exp(last) * jnp.sum(state * later, axis=0, keepdims=True)
        d_last = jnp.sum(ends, axis=1, keepdims=True)
        spread = jnp.broadcast_to(d_total, (CHUNK, CHUNK))
        d_glog = raw(tri3, jnp.concatenate(split3(spread), axis=0), NN) + d_last
        d_decay = -scale * d_glog * column[:, 3:4]
        scale_sum = scale_sum + d_glog * column
        bias_sum = bias_sum + d_decay
        d_all[here, 512:] = jnp.where(
            cols == 0, d_beta * beta * (1.0 - beta), jnp.where(cols == 1, d_decay, 0.0)
        ).astype(bf16)
        q_hat, k_hat = queries * 128**0.5, keys
        d_q = (rq * 128**-0.5) * (d_queries - q_hat * jnp.sum(q_hat * d_queries, axis=-1, keepdims=True))
        d_k = rk * (d_keys - k_hat * jnp.sum(k_hat * d_keys, axis=-1, keepdims=True))
        d_v = beta * right
        conv = conv_in[here, :]
        sig = jax.nn.sigmoid(conv)
        ext[here, :] = jnp.concatenate([d_q, d_k, d_v], axis=1) * (sig * (1.0 + conv * (1.0 - sig)))
    sums_out[0:1, :] += jnp.sum(scale_sum, axis=0, keepdims=True)
    sums_out[1:2, :] += jnp.sum(bias_sum, axis=0, keepdims=True)
    mixed = mixed_in[...].astype(f32)
    d_mixed = jnp.zeros((ROWS, 384), f32)
    for lag in range(CONV):
        moved = ext[CONV - 1 - lag : CONV - 1 - lag + ROWS, :]
        d_mixed = d_mixed + taps[lag : lag + 1, :] * moved
        taps_out[lag : lag + 1, :] += jnp.sum(mixed * moved, axis=0, keepdims=True)
    d_all[:, :384] = d_mixed.astype(bf16)
    d_all[:, 384:512] = gate_in[...]
    ext[ROWS : ROWS + 8, :] = ext[0:8, :]
    hidden = hidden_in[...]
    unit_out[...] += raw(hidden, d_all[:, :512], TN)
    logits_out[...] += raw(d_all[:, 512:], hidden, TN)[:8]
    first = numbers[0] < 0.5
    for at in range(GROUP):
        product = raw(d_all[at * CHUNK : (at + 1) * CHUNK, :], held[...], NT)
        low, high = product[:64], product[64:]
        keep_out[at] = jnp.where(first, low, high)
        give_out[at] = jnp.where(first, high, low).astype(bf16)

    @pl.when(step == 16 // GROUP - 1)
    def _():
        low_out[...] = unit_out[...].astype(bf16)


def backward_call(numbers, places, taps, *arrays):
    steps = 16 // GROUP
    shape = jax.ShapeDtypeStruct
    blocks = lambda width: pl.BlockSpec((ROWS, width), lambda i: (steps - 1 - i, 0))
    halves = pl.BlockSpec((GROUP, 64, 1024), lambda i: (steps - 1 - i, 0, 0))
    lines = pl.BlockSpec((1, GROUP, 128), lambda i: (steps - 1 - i, 0, 0))
    whole = lambda *dims: pl.BlockSpec(dims, lambda i: (0,) * len(dims))
    return pl.pallas_call(
        backward_kernel,
        grid=(steps,),
        in_specs=[pl.BlockSpec(memory_space=pltpu.SMEM)] * 2
        + [whole(4, 384), blocks(384)]
        + [blocks(128)] * 7
        + [blocks(384), blocks(128), blocks(128)]
        + [lines] * 4
        + [blocks(1024), blocks(128)]
        + [whole(256, 640)] * 4,
        out_specs=[halves, halves, whole(1024, 512), whole(1024, 512), whole(8, 1024), whole(8, 384), whole(8, 128)],
        out_shape=[
            shape((16, 64, 1024), f32),
            shape((16, 64, 1024), bf16),
            shape((1024, 512), f32),
            shape((1024, 512), bf16),
            shape((8, 1024), f32),
            shape((8, 384), f32),
            shape((8, 128), f32),
        ],
        scratch_shapes=[
            pltpu.VMEM((128, 128), f32),
            pltpu.VMEM((ROWS + 8, 384), f32),
            pltpu.VMEM((ROWS, 640), bf16),
            pltpu.VMEM((1024, 640), bf16),
        ],
        compiler_params=pltpu.CompilerParams(
            dimension_semantics=("arbitrary",), vmem_limit_bytes=52 * 1024 * 1024
        ),
        cost_estimate=cost(36),
        name="delta_backward",
    )(numbers, places, taps, *arrays)


def row_to_square(row):
    return jnp.broadcast_to(row, (CHUNK, CHUNK)).T


def head_rates(mine, theirs, at):
    squares = mine[0, at : at + 1, :] + theirs[0, at : at + 1, :]
    return row_to_square(lax.rsqrt(squares / 256.0 + epsilon))


def gate_kernel(heads, gate, mine, theirs, gain, out):
    for at in range(GROUP):
        here = slice(at * CHUNK, (at + 1) * CHUNK)
        normed = heads[here, :] * head_rates(mine, theirs, at)
        out[here, :] = (normed * gain[...] * silu(gate[here, :])).astype(bf16)


def specs(*widths):
    found = []
    for width in widths:
        if width == "rows":
            found.append(pl.BlockSpec((1, GROUP, 128), lambda i: (i, 0, 0)))
        elif width == "tokens":
            found.append(pl.BlockSpec((GROUP, 64, 1024), lambda i: (i, 0, 0)))
        elif width == "smem":
            found.append(pl.BlockSpec(memory_space=pltpu.SMEM))
        elif isinstance(width, tuple):
            found.append(pl.BlockSpec(width, lambda i, dims=len(width): (0,) * dims))
        else:
            found.append(pl.BlockSpec((ROWS, width), lambda i: (i, 0)))
    return found


def cost(microseconds):
    return pl.CostEstimate(flops=microseconds * 10**9, bytes_accessed=microseconds * 3 * 10**6, transcendentals=0)


def params():
    return pltpu.CompilerParams(dimension_semantics=("arbitrary",), vmem_limit_bytes=52 * 1024 * 1024)


def gate_call(heads, gate, mine, theirs, gain):
    return pl.pallas_call(
        gate_kernel,
        grid=(16 // GROUP,),
        in_specs=specs(128, 128, "rows", "rows", (1, 128)),
        out_specs=specs(128)[0],
        out_shape=jax.ShapeDtypeStruct((2048, 128), bf16),
        compiler_params=params(),
        cost_estimate=cost(3),
        name="gate",
    )(heads, gate, mine, theirs, gain)


def middle_kernel(numbers, gated, tokens, mine, theirs, gain, middle_out, hidden_out):
    core = numbers[0]
    for at in range(2):
        line = tokens[at].astype(f32)
        for weight, parity in ((mine, core), (theirs, 1 - core)):
            found = [gated[at * 16 + numbers[2 + grp] * 4 + parity * 2 + half] for grp in range(4) for half in range(2)]
            line = line + raw(jnp.concatenate(found, axis=1), weight[...], NN)
        rows = slice(at * 64, at * 64 + 64)
        middle_out[rows, :] = line
        rate = lax.rsqrt(jnp.mean(line * line, axis=-1, keepdims=True) + epsilon)
        hidden_out[rows, :] = (line * rate * gain[...]).astype(bf16)


def middle_call(places, gated, tokens, mine, theirs, gain):
    shape = jax.ShapeDtypeStruct
    return pl.pallas_call(
        middle_kernel,
        in_specs=[pl.BlockSpec(memory_space=pltpu.SMEM)] + [pl.BlockSpec(memory_space=pltpu.VMEM)] * 5,
        out_shape=[shape((128, 1024), f32), shape((128, 1024), bf16)],
        compiler_params=pltpu.CompilerParams(vmem_limit_bytes=52 * 1024 * 1024),
        cost_estimate=cost(4),
        name="middle",
    )(places, gated, tokens, mine, theirs, gain)


def d_gated_kernel(places, grads, mine, theirs, out):
    core = places[0]
    for weight, parity in ((mine, core), (theirs, 1 - core)):
        found = raw(grads[...], weight[...], NT)
        for seq in range(2):
            for grp in range(4):
                for half in range(2):
                    at = (grp * 2 + half) * 128
                    to = seq * 16 + places[2 + grp] * 4 + parity * 2 + half
                    out[to] = found[seq * 64 : seq * 64 + 64, at : at + 128]


def d_gated_call(places, grads, mine, theirs):
    return pl.pallas_call(
        d_gated_kernel,
        in_specs=[pl.BlockSpec(memory_space=pltpu.SMEM)] + [pl.BlockSpec(memory_space=pltpu.VMEM)] * 3,
        out_shape=jax.ShapeDtypeStruct((32, 64, 128), f32),
        compiler_params=pltpu.CompilerParams(vmem_limit_bytes=52 * 1024 * 1024),
        cost_estimate=cost(3),
        name="d_gated",
    )(places, grads, mine, theirs)


def output_weights_kernel(
    left_0, left_1, left_2, left_3, grads_0, grads_1, grads_2, grads_3, out
):
    grads = jnp.concatenate([grads_0[...], grads_1[...], grads_2[...], grads_3[...]], axis=0)
    for parity in range(2):
        for half in range(2):
            left = [side[seq, parity, half] for side in (left_0, left_1, left_2, left_3) for seq in range(2)]
            found = raw(jnp.concatenate(left, axis=0), grads, TN).astype(bf16)
            for part in range(8):
                for block in range(8):
                    piece = found[part * 16 : part * 16 + 16, block * 128 : block * 128 + 128]
                    at = parity * 128 + block * 16
                    out[half * 8 + part, at : at + 16, :] = piece


def output_weights_call(*arrays):
    return pl.pallas_call(
        output_weights_kernel,
        in_specs=[pl.BlockSpec(memory_space=pltpu.VMEM)] * 8,
        out_shape=jax.ShapeDtypeStruct((16, 256, 128), bf16),
        compiler_params=pltpu.CompilerParams(vmem_limit_bytes=52 * 1024 * 1024),
        cost_estimate=cost(3),
        name="output_weights",
    )(*arrays)


def ff_kernel(two, dy, weight, down, swi_out, grads_out, part_out):
    gateup = raw(two[...], weight[...], NN)
    d_swi = raw(dy[...], down[...], NT)
    gate, up = gateup[:, :384], gateup[:, 384:]
    sig = jax.nn.sigmoid(gate)
    active = gate * sig
    swi_out[...] = (active * up).astype(bf16)
    grads_out[:, :384] = (d_swi * up * (sig * (1.0 + gate * (1.0 - sig)))).astype(bf16)
    grads_out[:, 384:] = (d_swi * active).astype(bf16)
    part_out[...] = raw(grads_out[...], weight[...], NT)


def ff_call(two, dy, weight, down):
    shape = jax.ShapeDtypeStruct
    rows = lambda width: pl.BlockSpec((256, width), lambda i: (i, 0))
    whole = lambda *dims: pl.BlockSpec(dims, lambda i: (0, 0))
    return pl.pallas_call(
        ff_kernel,
        grid=(2,),
        in_specs=[rows(1024), rows(1024), whole(1024, 768), whole(384, 1024)],
        out_specs=[rows(384), rows(768), rows(1024)],
        out_shape=[shape((512, 384), bf16), shape((512, 768), bf16), shape((512, 1024), f32)],
        compiler_params=params(),
        cost_estimate=cost(5),
        name="ff",
    )(two, dy, weight, down)


def ff_sum_kernel(two, dy, weight, down, added, swi_out, grads_out, low_out, own_out, part):
    ff_kernel(two, dy, weight, down, swi_out, grads_out, part)
    total = part[...] + added[...]
    low_out[...] = total.astype(bf16)

    @pl.when(pl.program_id(0) == 0)
    def _():
        own_out[...] = total[:128]


def ff_sum_call(two, dy, weight, down, added):
    shape = jax.ShapeDtypeStruct
    rows = lambda width: pl.BlockSpec((256, width), lambda i: (i, 0))
    whole = lambda *dims: pl.BlockSpec(dims, lambda i: (0, 0))
    return pl.pallas_call(
        ff_sum_kernel,
        grid=(2,),
        in_specs=[rows(1024), rows(1024), whole(1024, 768), whole(384, 1024), rows(1024)],
        out_specs=[rows(384), rows(768), rows(1024), whole(128, 1024)],
        out_shape=[
            shape((512, 384), bf16),
            shape((512, 768), bf16),
            shape((512, 1024), bf16),
            shape((128, 1024), f32),
        ],
        scratch_shapes=[pltpu.VMEM((256, 1024), f32)],
        compiler_params=params(),
        cost_estimate=cost(5),
        name="ff_sum",
    )(two, dy, weight, down, added)


def gate_back_kernel(
    d_gated, heads, gate, sq_mine, sq_theirs, gain,
    normed_out, gate_out, inner_out, head_out,
):
    @pl.when(pl.program_id(0) == 0)
    def _():
        head_out[...] = jnp.zeros_like(head_out)

    ones = jnp.ones((8, 256), bf16)
    for at in range(GROUP):
        here = slice(at * CHUNK, (at + 1) * CHUNK)
        grads = d_gated[here, :]
        value = heads[here, :]
        normed = value * head_rates(sq_mine, sq_theirs, at)
        logits = gate[here, :]
        sig = jax.nn.sigmoid(logits)
        active = logits * sig
        head_out[0:1, :] += jnp.sum(grads * normed * active, axis=0, keepdims=True)
        gained = grads * gain[...]
        gate_out[here, :] = (gained * normed * (sig * (1.0 + logits * (1.0 - sig)))).astype(bf16)
        d_normed = gained * active
        normed_out[here, :] = d_normed
        product = raw(ones, jnp.concatenate(split(d_normed * value), axis=1), NT)
        inner_out[0, at : at + 1, :] = product[0:1, :]


def gate_back_call(*arrays):
    shape = jax.ShapeDtypeStruct
    return pl.pallas_call(
        gate_back_kernel,
        grid=(16 // GROUP,),
        in_specs=specs(128, 128, 128, "rows", "rows", (1, 128)),
        out_specs=specs(128, 128, "rows", (8, 128)),
        out_shape=[
            shape((2048, 128), f32),
            shape((2048, 128), bf16),
            shape((16 // GROUP, GROUP, 128), f32),
            shape((8, 128), f32),
        ],
        compiler_params=params(),
        cost_estimate=cost(4),
        name="gate_back",
    )(*arrays)


def ff_weights_kernel(two_0, two_1, grads_0, grads_1, swi_0, swi_1, dy_0, dy_1, out):
    grp = pl.program_id(0)
    found = raw(two_0[...], grads_0[...], TN) + raw(two_1[...], grads_1[...], TN)
    for chip in range(16):
        for part in range(6):
            at = pl.multiple_of(grp * 96 + part * 16, 16)
            block = found[chip * 16 : chip * 16 + 16, part * 128 : part * 128 + 128]
            out[chip, pl.ds(at, 16), :] = block
    found = raw(swi_0[...], dy_0[...], TN) + raw(swi_1[...], dy_1[...], TN)
    for chip in range(16):
        for part in range(2):
            at = pl.multiple_of(384 + grp * 64 + part * 32, 32)
            if chip < 11:
                block = found[chip * 32 : chip * 32 + 32, part * 128 : part * 128 + 128]
            else:
                block = jnp.zeros((32, 128), f32)
            out[chip, pl.ds(at, 32), :] = block


def ff_weights_call(*arrays):
    columns = pl.BlockSpec((512, 256), lambda i: (0, i))
    whole = lambda width: pl.BlockSpec((512, width), lambda i: (0, 0))
    return pl.pallas_call(
        ff_weights_kernel,
        grid=(4,),
        in_specs=[columns] * 2 + [whole(768)] * 2 + [whole(384)] * 2 + [columns] * 2,
        out_specs=pl.BlockSpec((16, 640, 128), lambda i: (0, 0, 0)),
        out_shape=jax.ShapeDtypeStruct((16, 640, 128), f32),
        compiler_params=params(),
        cost_estimate=cost(7),
        name="ff_weights",
    )(*arrays)


def ff_grads_kernel(numbers, places, mine, theirs, weight, gain, gateup_out, down_out, output_out, gain_out):
    step = pl.program_id(0)
    first = numbers[0] < 0.5

    def piece(core, chip, at, size):
        one, two = mine[chip, pl.ds(at, size), :], theirs[chip, pl.ds(at, size), :]
        return (jnp.where(first, one, two) if core == 0 else jnp.where(first, two, one)).astype(f32)

    for chip in range(4):
        rows = slice(chip * 16, chip * 16 + 16)
        total = jnp.zeros((16, 128), f32)
        for half in range(2):
            found = []
            for grp in range(4):
                for core in range(2):
                    for part in range(3):
                        at = pl.multiple_of(places[2 + grp] * 96 + half * 48 + part * 16, 16)
                        block = piece(core, chip, at, 16)
                        found.append(block if part < 2 else block[:, :96])
            line = jnp.concatenate(found, axis=1)
            gateup_out[rows, half * FF : (half + 1) * FF] = line
            product = line * weight[rows, half * FF : (half + 1) * FF].astype(f32)
            for part in range(FF // 128):
                total = total + product[:, part * 128 : part * 128 + 128]
        total = jnp.sum(total, axis=1, keepdims=True)
        gain_out[rows, :] = jnp.broadcast_to(total, (16, 128)) / gain[rows, :].astype(f32)

        for core in range(2):
            at = pl.multiple_of(core * 256 + (step * 4 + chip) * 16, 16)
            for part in range(8):
                output_out[pl.ds(at, 16), part * 128 : part * 128 + 128] = piece(core, chip, 640 + part * 16, 16)

        @pl.when(step * 4 + chip < 11)
        def _():
            for core in range(2):
                at = pl.multiple_of(core * 352 + (step * 4 + chip) * 32, 8)
                for part in range(8):
                    down_out[pl.ds(at, 32), part * 128 : part * 128 + 128] = piece(core, chip, 384 + part * 32, 32)


def ff_grads_call(numbers, places, mine, theirs, weight, gain):
    shape = jax.ShapeDtypeStruct
    return pl.pallas_call(
        ff_grads_kernel,
        grid=(4,),
        in_specs=[
            pl.BlockSpec(memory_space=pltpu.SMEM),
            pl.BlockSpec(memory_space=pltpu.SMEM),
            pl.BlockSpec((4, 768, 128), lambda i: (i, 0, 0)),
            pl.BlockSpec((4, 768, 128), lambda i: (i, 0, 0)),
            pl.BlockSpec((64, 2 * FF), lambda i: (i, 0)),
            pl.BlockSpec((64, 128), lambda i: (i, 0)),
        ],
        out_specs=[
            pl.BlockSpec((64, 2 * FF), lambda i: (i, 0)),
            pl.BlockSpec((704, 1024), lambda i: (0, 0)),
            pl.BlockSpec((512, 1024), lambda i: (0, 0)),
            pl.BlockSpec((64, 128), lambda i: (i, 0)),
        ],
        out_shape=[
            shape((256, 2 * FF), f32),
            shape((704, 1024), f32),
            shape((512, 1024), f32),
            shape((256, 128), f32),
        ],
        compiler_params=params(),
        cost_estimate=cost(8),
        name="ff_grads",
    )(numbers, places, mine, theirs, weight, gain)


def mixer_grads_kernel(numbers, mine, theirs, weight, gate_weight, mixer_out, gate_out, sum_out):
    first = numbers[0] < 0.5
    for head in range(8):
        one, two = mine[head], theirs[head]
        for core in range(2):
            piece = jnp.where(first, one, two) if core == 0 else jnp.where(first, two, one)
            piece = piece.astype(f32)
            rows = slice(core * 64, core * 64 + 64)
            mixer_out[rows, head * 128 : head * 128 + 128] = piece[:64]
            mixer_out[rows, 1024 + head * 128 : 1152 + head * 128] = piece[64:128]
            to = 2048 + head * 256 + core * 128
            mixer_out[:, to : to + 128] = piece[128:256]
            to = head * 256 + core * 128
            gate_out[:, to : to + 128] = piece[256:384]
    total = jnp.sum(mixer_out[...] * weight[...].astype(f32), axis=1, keepdims=True)
    total = total + jnp.sum(gate_out[...] * gate_weight[...].astype(f32), axis=1, keepdims=True)
    sum_out[...] = jnp.broadcast_to(total, (128, 128))


def mixer_grads_call(numbers, mine, theirs, weight, gate_weight):
    shape = jax.ShapeDtypeStruct
    return pl.pallas_call(
        mixer_grads_kernel,
        grid=(2,),
        in_specs=[
            pl.BlockSpec(memory_space=pltpu.SMEM),
            pl.BlockSpec((8, 384, 128), lambda i: (i, 0, 0)),
            pl.BlockSpec((8, 384, 128), lambda i: (i, 0, 0)),
            pl.BlockSpec((128, 4096), lambda i: (i, 0)),
            pl.BlockSpec((128, 2048), lambda i: (i, 0)),
        ],
        out_specs=[
            pl.BlockSpec((128, 4096), lambda i: (i, 0)),
            pl.BlockSpec((128, 2048), lambda i: (i, 0)),
            pl.BlockSpec((128, 128), lambda i: (i, 0)),
        ],
        out_shape=[shape((256, 4096), f32), shape((256, 2048), f32), shape((256, 128), f32)],
        compiler_params=params(),
        cost_estimate=cost(4),
        name="mixer_grads",
    )(numbers, mine, theirs, weight, gate_weight)


def mm(left, right):
    return raw(left, right, NN)


def mm_t(left, right):
    return raw(left, right, NT)


def t_mm(left, right):
    return raw(left, right, TN)


def other_core(value):
    return lax.ppermute(value, "ctx", OTHER_CORE)


def other_seq(value):
    return lax.ppermute(value, "ctx", OTHER_SEQ)


def along_grp(value, steps):
    return lax.ppermute(value, "grp", [(at, (at + steps) % 4) for at in range(4)])


def from_grp(value):
    return [value] + [along_grp(value, steps) for steps in (1, 2, 3)]


def in_grp_order(pieces, place):
    turned = [pieces[0], pieces[3], pieces[2], pieces[1]]
    doubled = jnp.stack(turned + turned[:3])
    return lax.dynamic_slice_in_dim(doubled, (4 - place) % 4, 4, axis=0)


def exchange_grp(value, place):
    part = lambda steps: lax.dynamic_index_in_dim(value, (place + steps) % 4, 0, False)
    return [part(0)] + [along_grp(part(steps), steps) for steps in (1, 2, 3)]


def sum_grp(value, place):
    mine, *others = exchange_grp(value.astype(bf16), place)
    total = lax.dynamic_index_in_dim(value, place, 0, False)
    for other in others:
        total = total + other.astype(f32)
    return total


def sum_chips(value):
    flat = value.reshape(-1, 128)
    return lax.psum_scatter(flat, "ctx", scatter_dimension=0, tiled=True, axis_index_groups=CHIPS)


def over_chips(value):
    return lax.all_to_all(value, "ctx", 0, 0, axis_index_groups=CHIPS)


def body(
    block_input,
    seq_lengths,
    in_gain,
    w_mixer,
    conv_weight,
    w_rates,
    decay_scale,
    decay_bias,
    w_outgate,
    head_gain,
    w_output,
    mlp_gain,
    w_gateup,
    w_down,
    cotangent,
):
    place = lax.axis_index("ctx")
    grp = lax.axis_index("grp")
    core = place % 2
    head = (place % 16) // 2
    seq = place // 16
    unit = place % 16

    x_all = jnp.repeat(block_input, 8, axis=0)
    w_mixer_one, w_output_one, x_all = lax.optimization_barrier((w_mixer, w_output, x_all))
    x_mine = over_chips(x_all)

    def unit_columns(value):
        q_part = lax.dynamic_slice_in_dim(value, head * 128, 128, axis=1)
        k_part = lax.dynamic_slice_in_dim(value, 1024 + head * 128, 128, axis=1)
        v_part = lax.dynamic_slice_in_dim(value, 2048 + unit * 128, 128, axis=1)
        return [q_part, k_part, v_part]

    small = jnp.concatenate(
        [
            conv_weight.reshape(-1),
            in_gain,
            mlp_gain,
            head_gain,
            decay_scale,
            decay_bias,
            jnp.zeros((188,), bf16),
        ]
    ).reshape(256, 19)
    unit_part = jnp.concatenate(
        unit_columns(w_mixer_one)
        + [
            lax.dynamic_slice_in_dim(w_outgate, unit * 128, 128, axis=1),
            lax.dynamic_slice_in_dim(w_rates, head, 1, axis=1),
            lax.dynamic_slice_in_dim(w_rates, 8 + head, 1, axis=1),
            small,
            jnp.zeros((256, 107), bf16),
        ],
        axis=1,
    )
    w_unit = from_grp(unit_part)
    small = in_grp_order([piece[:, 514:533] for piece in w_unit], grp).reshape(4, -1)
    conv_full = small[:, :4096].reshape(4, 4, 1024).transpose(1, 0, 2).reshape(4, 4096).astype(f32)
    gain_one = small[:, 4096:4352].reshape(1, 1024).astype(f32)
    gain_two = small[:, 4352:4608].reshape(1, 1024).astype(f32)
    head_full = small[:, 4608:4672].reshape(1, 256).astype(f32)
    scale_full = small[:, 4672:4674].reshape(8).astype(f32)
    bias_full = small[:, 4674:4676].reshape(8).astype(f32)

    taps = jnp.concatenate(unit_columns(conv_full), axis=1)
    scale = lax.dynamic_index_in_dim(scale_full, head, 0, False)
    bias = lax.dynamic_index_in_dim(bias_full, head, 0, False)
    head_half = lax.dynamic_slice_in_dim(head_full, core * 128, 128, axis=1)
    numbers = jnp.stack([core.astype(f32), bias, jnp.exp(scale), jnp.zeros((), f32)])

    def ff_columns(owner):
        at = owner * 704 + core * 352
        gate = lax.dynamic_slice_in_dim(w_gateup, at, 352, axis=1)
        up = lax.dynamic_slice_in_dim(w_gateup, FF + at, 352, axis=1)
        fill = jnp.zeros((256, 32), bf16)
        return jnp.concatenate([gate, fill, up, fill], axis=1)

    gateup_pieces = jnp.stack([ff_columns(owner) for owner in range(4)])
    w_dn = jnp.concatenate(
        [lax.dynamic_slice_in_dim(w_down, core * 352, 352, axis=0), jnp.zeros((32, 1024), bf16)], axis=0
    )
    output_half = lax.dynamic_slice_in_dim(w_output_one, core * 256, 256, axis=0)

    positions = place * 64 + lax.broadcasted_iota(jnp.int32, (2, 64), 1)
    valid = (positions < seq_lengths[:, None]).astype(f32)[..., None]
    inputs_rows = block_input.astype(f32).reshape(128, 1024)
    r_one = lax.rsqrt(jnp.mean(inputs_rows * inputs_rows, axis=-1, keepdims=True) + epsilon)
    dy = (cotangent.astype(f32) * valid).reshape(128, 1024)
    dy_low = dy.astype(bf16)

    def to_wide(tokens):
        mine = jnp.concatenate(from_grp(tokens), axis=0)
        return mine, other_core(mine)

    def over_cores(mine, theirs, sent):
        mine = mine + other_core(theirs.astype(sent)).astype(f32)
        return mine[:128], mine.reshape(4, 128, 1024).astype(bf16)

    def over_grp(total, low):
        for steps in (1, 2, 3):
            total = total + along_grp(low[steps], -steps).astype(f32)
        return total

    places = jnp.stack([core, head] + [(grp - steps) % 4 for steps in range(4)])
    output_pieces = from_grp(output_half)
    gateup_pieces, w_dn, w_unit, output_pieces, numbers, places, gain_one, taps, x_mine = lax.optimization_barrier(
        (gateup_pieces, w_dn, w_unit, output_pieces, numbers, places, gain_one, taps, x_mine)
    )
    x_theirs = other_core(x_mine)
    gateup_pieces = lax.all_to_all(gateup_pieces, "grp", 0, 0)
    (
        hidden_one, mixed_in, outgate, conv, columns, inverse, from_state, updates, scores, moves, states, heads_out,
        squares,
    ) = forward_call(numbers, places, x_mine, x_theirs, gain_one, w_unit, taps)
    heads_out, squares, gateup_pieces = lax.optimization_barrier((heads_out, squares, gateup_pieces))
    squares_theirs = other_core(squares)
    gated = gate_call(heads_out, outgate, squares, squares_theirs, head_half)

    dy_low, output_pieces, gated = lax.optimization_barrier((dy_low, output_pieces, gated))
    gated_tokens = lax.all_to_all(gated.reshape(32, 64, 128), "ctx", 0, 0)
    dy_mine = jnp.concatenate(from_grp(dy_low), axis=0)
    output_mine = jnp.concatenate(output_pieces, axis=0)
    output_theirs = other_core(output_mine)
    gated_tokens, dy_mine = lax.optimization_barrier((gated_tokens, dy_mine))
    dy_theirs = other_core(dy_mine)
    middle, hidden_two = middle_call(places, gated_tokens, block_input, output_mine, output_theirs, gain_two)
    r_two = lax.rsqrt(jnp.mean(middle * middle, axis=-1, keepdims=True) + epsilon)
    two_mine, two_theirs = to_wide(hidden_two)
    w_gu = gateup_pieces.reshape(1024, 768)
    swi_theirs, grads_theirs, part_theirs = ff_call(two_theirs, dy_theirs, w_gu, w_dn)
    by_grp = exchange_grp(gated_tokens.reshape(2, 4, 2, 2, 64, 128).transpose(1, 0, 2, 3, 4, 5), grp)
    swi_mine, grads_mine, part_low, part_own = ff_sum_call(two_mine, dy_mine, w_gu, w_dn, other_core(part_theirs))
    part_low, part_own, swi_mine, grads_mine, by_grp = lax.optimization_barrier(
        (part_low, part_own, swi_mine, grads_mine, by_grp)
    )
    g_ff = ff_weights_call(
        two_mine, two_theirs, grads_mine, grads_theirs, swi_mine, swi_theirs, dy_mine, dy_theirs
    )
    dhidden_two = over_grp(part_own, part_low.reshape(4, 128, 1024))
    scaled = dhidden_two * gain_two
    dmiddle = dy + r_two * scaled - middle * r_two**3 * jnp.mean(scaled * middle, axis=-1, keepdims=True)
    dmix = dmiddle.astype(bf16)
    dmix, g_ff = lax.optimization_barrier((dmix, g_ff))
    g_ff = sum_chips(g_ff)
    d_gated = d_gated_call(places, dmix, output_mine, output_theirs)
    dmix, d_gated = lax.optimization_barrier((dmix, d_gated))
    d_gated = lax.all_to_all(d_gated, "ctx", 0, 0)

    dmix_pieces, d_gated = lax.optimization_barrier((from_grp(dmix), d_gated))
    g_output = output_weights_call(*by_grp, *dmix_pieces)
    d_gated, g_output = lax.optimization_barrier((d_gated, g_output))
    g_output = over_chips(g_output)

    d_normed, d_outgate, inner, g_head = gate_back_call(
        d_gated.reshape(2048, 128), heads_out, outgate, squares, squares_theirs, head_half
    )
    inner_theirs = other_core(inner)
    keep, give, g_unit, g_unit_low, g_rates, g_taps, g_sums = backward_call(
        numbers, places, taps, conv, columns, inverse, from_state, updates, scores, moves, states, mixed_in,
        d_normed, heads_out, squares, squares_theirs, inner, inner_theirs, hidden_one, d_outgate, *w_unit,
    )

    give, g_output = lax.optimization_barrier((give, g_output))
    give_theirs = other_core(give)
    d_sent = (keep + give_theirs.astype(f32)).astype(bf16)
    g_ff, g_output, g_unit_low, d_sent = lax.optimization_barrier((g_ff, g_output, g_unit_low, d_sent))
    d_tokens = over_chips(d_sent)
    g_unit_pieces = exchange_grp(g_unit_low.reshape(4, 256, 512), grp)[1:]
    g_output = g_output.astype(f32).sum(axis=0).reshape(2, 128, 128)
    g_output_theirs = other_core(lax.dynamic_index_in_dim(g_output, 1 - core, 0, False).astype(bf16))
    g_output = lax.dynamic_index_in_dim(g_output, core, 0, False) + g_output_theirs.astype(f32)
    g_gu = exchange_grp(g_ff[:384].astype(bf16).reshape(4, 96, 128), grp)
    early = jnp.concatenate(g_gu + [g_ff[384:].astype(bf16), g_output.astype(bf16)], axis=0)
    g_rates = g_rates[:2].reshape(2, 4, 2, 128).transpose(1, 0, 2, 3).reshape(4, 4, 128)
    shared = jnp.concatenate(
        [g_taps[:4].reshape(12, 128), g_head[:1], g_sums[:2], jnp.zeros((5, 128), f32)], axis=0
    )
    g_small = jnp.concatenate([jnp.broadcast_to(shared, (4, 20, 128)), g_rates], axis=1)
    g_small = exchange_grp(g_small, grp)
    g_unit_pieces, g_small, d_tokens = lax.optimization_barrier((g_unit_pieces, g_small, d_tokens))
    early_mine = lax.all_gather(early, "ctx", axis_index_groups=CHIPS)
    early_theirs = other_core(early_mine)
    grad_gateup, grad_down, grad_output, mlp_sums = ff_grads_call(
        numbers, places, early_mine, early_theirs, w_gateup, jnp.broadcast_to(mlp_gain[:, None], (256, 128))
    )

    g_small = sum(g_small)
    g_sum = lax.dynamic_index_in_dim(g_unit.reshape(4, 256, 512), grp, 0, False)
    for other in g_unit_pieces:
        g_sum = g_sum + other.astype(f32)
    g_sum = g_sum.reshape(2, 128, 512)

    dhidden_one = d_tokens.astype(f32)
    dhidden_one = dhidden_one.reshape(2, 8, 64, 1024).sum(axis=1).reshape(128, 1024)
    scaled = dhidden_one * gain_one
    input_grad = (
        dmiddle + r_one * scaled - inputs_rows * r_one**3 * jnp.mean(scaled * inputs_rows, axis=-1, keepdims=True)
    )

    mine = lax.dynamic_index_in_dim(g_sum, seq, 0, False)
    given = lax.dynamic_index_in_dim(g_sum, 1 - seq, 0, False).astype(bf16)
    mine = mine + other_seq(given).astype(f32)
    halves = mine[:, :256].reshape(2, 64, 256)
    qk_mine = lax.dynamic_index_in_dim(halves, core, 0, False)
    qk_given = lax.dynamic_index_in_dim(halves, 1 - core, 0, False).astype(bf16)
    qk_mine = qk_mine + other_core(qk_given).astype(f32)
    late = [qk_mine[:, :128], qk_mine[:, 128:], mine[:, 256:384], mine[:, 384:]]
    late = jnp.concatenate(late, axis=0).astype(bf16)
    small_high = lax.optimization_barrier(g_small.astype(bf16))
    small_low = (g_small - small_high.astype(f32)).astype(bf16)
    late = jnp.concatenate([late, small_high, small_low], axis=0)
    late, swi_mine, swi_theirs = lax.optimization_barrier((late, swi_mine, swi_theirs))
    late_mine = over_chips(jnp.broadcast_to(late, (16,) + late.shape))
    block_out = middle + over_grp(*over_cores(mm(swi_mine, w_dn), mm(swi_theirs, w_dn), bf16))
    block_output = (block_out.reshape(2, 64, 1024) * valid).astype(bf16)
    late_mine, block_output, input_grad = lax.optimization_barrier((late_mine, block_output, input_grad))
    late_theirs = other_core(late_mine)
    grad_mixer, grad_outgate, mixer_sums = mixer_grads_call(numbers, late_mine, late_theirs, w_mixer, w_outgate)
    small_one = (late_mine[:, 384:408].astype(f32) + late_mine[:, 408:].astype(f32)).reshape(2, 8, 24, 128)
    small_two = (late_theirs[:, 384:408].astype(f32) + late_theirs[:, 408:].astype(f32)).reshape(2, 8, 24, 128)
    small_one, small_two = small_one.sum(axis=0), small_two.sum(axis=0)
    both = small_one + small_two
    g_low = jnp.where(core == 0, small_one, small_two)
    g_high = jnp.where(core == 0, small_two, small_one)
    taps_at = lambda value, at: value[:, :12].reshape(8, 4, 3, 128)[:, :, at].transpose(1, 0, 2).reshape(4, 1024)
    taps_v = jnp.stack([g_low[:, :12], g_high[:, :12]], axis=1).reshape(8, 2, 4, 3, 128)[:, :, :, 2]
    taps_v = taps_v.transpose(2, 0, 1, 3).reshape(4, 2048)
    grad_conv = jnp.concatenate([taps_at(both, 0), taps_at(both, 1), taps_v], axis=1)
    grad_conv = lax.dynamic_slice_in_dim(grad_conv, grp * 1024, 1024, axis=1)
    grad_head = jnp.concatenate([g_low[:, 12].sum(axis=0), g_high[:, 12].sum(axis=0)])
    grad_head = lax.dynamic_slice_in_dim(grad_head, grp * 64, 64, axis=0)
    grad_scale = lax.dynamic_slice_in_dim(both[:, 13, 1], grp * 2, 2, axis=0)
    grad_bias = lax.dynamic_slice_in_dim(both[:, 14, 1], grp * 2, 2, axis=0)
    grad_rates = both[:, 20:].reshape(8, 2, 256).transpose(1, 0, 2).reshape(16, 256).T
    grad_in_gain = (
        mixer_sums[:, 0]
        + jnp.sum(grad_rates * w_rates.astype(f32), axis=1)
    ) / in_gain.astype(f32)

    return (
        block_output,
        input_grad.reshape(2, 64, 1024),
        grad_in_gain,
        grad_mixer,
        grad_conv,
        grad_rates,
        grad_scale,
        grad_bias,
        grad_outgate,
        grad_head,
        grad_output,
        mlp_sums[:, 0],
        grad_gateup,
        grad_down,
    )


def solution(mesh):
    tokens = P("grp", "ctx", None)
    rows = P("grp", None)
    one = P("grp")
    taps = P(None, "grp")
    return jax.shard_map(
        body,
        mesh=mesh,
        in_specs=(tokens, one, one, rows, taps, rows, one, one, rows, one, rows, one, rows, rows, tokens),
        out_specs=(tokens, tokens, one, rows, taps, rows, one, one, rows, one, rows, one, rows, rows),
        check_vma=False,
    )
```

```python
import jax
import jax.numpy as jnp
from jax import lax
from jax.experimental import pallas as pl
from jax.experimental.pallas import tpu as pltpu
from jax.sharding import PartitionSpec as P

f32 = jnp.float32
bf16 = jnp.bfloat16
epsilon = 1e-06
CONV = 4
CHUNK = 128
GROUP = 4
ROWS = CHUNK * GROUP

FF = 2816
WIDE_GROUP = 8
WIDE_ROWS = CHUNK * WIDE_GROUP
VMEM_LIMIT = 60 * 1024 * 1024

CHIPS = [[chip * 2 + core for chip in range(16)] for core in range(2)]
OTHER_CORE = [(place, place ^ 1) for place in range(32)]
OTHER_SEQ = [(place, place ^ 16) for place in range(32)]

NN = ((1,), (0,))
NT = ((1,), (1,))
TN = ((0,), (0,))


def raw(left, right, dims):
    return lax.dot_general(left, right, (dims, ((), ())), preferred_element_type=f32)


def split(value):
    high = value.astype(bf16)
    return high, (value - high.astype(f32)).astype(bf16)


def split3(value):
    high = value.astype(bf16)
    rest = value - high.astype(f32)
    mid = rest.astype(bf16)
    return high, mid, (rest - mid.astype(f32)).astype(bf16)


def dot3(left, right, dims):
    lefts = jnp.concatenate([left[0], left[0], left[1]], axis=dims[0][0])
    rights = jnp.concatenate([right[0], right[1], right[0]], axis=dims[1][0])
    return raw(lefts, rights, dims)


def stacked(*pairs, axis=0):
    return tuple(jnp.concatenate([pair[part] for pair in pairs], axis=axis) for part in (0, 1))


def square_iota():
    rows = lax.broadcasted_iota(jnp.int32, (CHUNK, CHUNK), 0)
    cols = lax.broadcasted_iota(jnp.int32, (CHUNK, CHUNK), 1)
    return rows, cols


def inverses(lowers, rows, cols):
    results = [
        jnp.where(rows == cols, 1.0, 0.0) - jnp.where((rows >> 1) == (cols >> 1), lower, 0.0) for lower in lowers
    ]
    level = 1
    while (1 << level) < CHUNK:
        mask = ((rows >> (level + 1)) == (cols >> (level + 1))) & ((rows >> level) != (cols >> level))
        held = [split(result) for result in results]
        parts = [split(jnp.where(mask, lower, 0.0)) for lower in lowers]
        inner = [split(dot3(part, pair, NN)) for part, pair in zip(parts, held)]
        results = [result - dot3(pair, part, NN) for result, pair, part in zip(results, held, inner)]
        level += 1
    return results


def silu(value):
    return value * jax.nn.sigmoid(value)


def softplus(value):
    return jnp.maximum(value, 0.0) + jnp.log1p(jnp.exp(-jnp.abs(value)))


def decay_matrix(total, rows, cols):
    across = total.T[2:3, :]
    return jnp.where(cols <= rows, jnp.exp(jnp.minimum(total[:, 2:3] - across, 0.0)), 0.0)


def unit_norms(active):
    q, k = active[:, :128], active[:, 128:256]
    rq = lax.rsqrt(jnp.sum(q * q, axis=-1, keepdims=True) + epsilon)
    rk = lax.rsqrt(jnp.sum(k * k, axis=-1, keepdims=True) + epsilon)
    return q, k, rq, rk


def block_of(places, steps):
    return pl.ds(pl.multiple_of(places[2 + steps] * 256, 256), 256)


def forward_kernel(
    numbers, places, mine, theirs, gain, weight_0, weight_1, weight_2, weight_3, taps,
    hidden_out, mixed_out, gate_out, conv_out, cols_out, inv_out, from_out, upd_out, score_out, move_out, state_out,
    heads_out, square_out,
    state, ext, held,
):
    step = pl.program_id(0)
    core, bias, scale = numbers[0], numbers[1], numbers[2]

    @pl.when(step == 0)
    def _():
        state[...] = jnp.zeros_like(state)
        ext[0:8, :] = jnp.zeros((8, 384), f32)
        for steps, weight in enumerate((weight_0, weight_1, weight_2, weight_3)):
            held[block_of(places, steps), :] = weight[...]

    first = core < 0.5
    for at in range(WIDE_GROUP):
        one, two = mine[at], theirs[at]
        x = jnp.concatenate([jnp.where(first, one, two), jnp.where(first, two, one)], axis=0).astype(f32)
        rate = lax.rsqrt(jnp.mean(x * x, axis=-1, keepdims=True) + epsilon)
        hidden_out[at * CHUNK : (at + 1) * CHUNK, :] = (x * rate * gain[...]).astype(bf16)
    projected = raw(hidden_out[...], held[...], NN)
    mixed = projected[:, :384].astype(bf16)
    mixed_out[...] = mixed
    gate_out[...] = projected[:, 384:512]
    rates = projected[:, 512:]
    ext[8 : 8 + WIDE_ROWS, :] = mixed.astype(f32)
    conv = taps[0:1, :] * ext[5 : 5 + WIDE_ROWS, :]
    for lag in range(1, CONV):
        conv = conv + taps[lag : lag + 1, :] * ext[5 + lag : 5 + lag + WIDE_ROWS, :]
    ext[0:8, :] = ext[WIDE_ROWS : WIDE_ROWS + 8, :]
    conv_out[...] = conv
    lanes = lax.broadcasted_iota(jnp.int32, (WIDE_ROWS, 128), 1)
    sums_in = jnp.broadcast_to(rates[:, 1:2], (WIDE_ROWS, 128)) + bias
    glog = -scale * softplus(sums_in)
    cols_all = jnp.where(lanes == 0, jax.nn.sigmoid(rates), jnp.where(lanes == 3, jax.nn.sigmoid(sums_in), glog))
    rows, cols = square_iota()
    tri = jnp.where(cols <= rows, 1.0, 0.0).astype(bf16)
    tri3 = jnp.concatenate([tri, tri, tri], axis=1)
    lane = lax.broadcasted_iota(jnp.int32, (CHUNK, CHUNK), 1)
    lowers, kept = [], []
    for at in range(WIDE_GROUP):
        here = slice(at * CHUNK, (at + 1) * CHUNK)
        q, k, rq, rk = unit_norms(silu(conv[here, :256]))
        queries, keys = q * (rq * 128**-0.5), k * rk
        values = silu(conv[here, 256:])
        column = cols_all[here]
        running = raw(tri3, jnp.concatenate(split3(column), axis=0), NN)
        column = jnp.where(lane == 2, running, column)
        cols_out[here, :] = column
        decay = decay_matrix(column, rows, cols)
        beta = column[:, 0:1]
        total = column[:, 2:3]
        growth = jnp.exp(total)
        last = total[CHUNK - 1 : CHUNK, :]
        keys_s = split(keys)
        queries_s = split(queries)
        products = dot3(stacked(keys_s, queries_s), keys_s, NT)
        lowers.append(jnp.where(cols < rows, decay, 0.0) * products[:CHUNK] * beta)
        scores = products[CHUNK:] * decay
        score_out[here, :] = scores
        right = split(jnp.concatenate([(beta * growth) * keys, beta * values], axis=1))
        ends = split(jnp.exp(last - total) * keys)
        kept.append((split(scores), right, ends, split(growth * queries), jnp.exp(last)))
    found = inverses(lowers, rows, cols)
    both = []
    for at in range(WIDE_GROUP):
        here = slice(at * CHUNK, (at + 1) * CHUNK)
        inv_out[here, :] = found[at]
        both.append(dot3(split(found[at]), kept[at][1], NN))
    maps = []
    for at in range(WIDE_GROUP):
        here = slice(at * CHUNK, (at + 1) * CHUNK)
        from_out[here, :] = both[at][:, :128]
        ended = dot3(kept[at][2], split(both[at]), TN)
        move = jnp.where(rows == cols, kept[at][4], 0.0) - ended[:, :128]
        move_out[here, :] = move
        maps.append((split(move), ended[:, 128:]))
    current = state[...]
    states = []
    for at in range(WIDE_GROUP):
        here = slice(at * CHUNK, (at + 1) * CHUNK)
        state_out[here, :] = current
        pair = split(current)
        states.append(pair)
        current = dot3(maps[at][0], pair, NN) + maps[at][1]
    state[...] = current
    ones = jnp.ones((8, 256), bf16)
    for at in range(WIDE_GROUP):
        here = slice(at * CHUNK, (at + 1) * CHUNK)
        product = dot3(stacked(split(both[at][:, :128]), kept[at][3]), states[at], NN)
        updates = both[at][:, 128:] - product[:CHUNK]
        upd_out[here, :] = updates
        heads = product[CHUNK:] + dot3(kept[at][0], split(updates), NN)
        heads_out[here, :] = heads
        squares = raw(ones, jnp.concatenate(split(heads * heads), axis=1), NT)
        square_out[0, at : at + 1, :] = squares[0:1, :]


def forward_call(numbers, places, mine, theirs, gain, weights, taps):
    steps = 16 // WIDE_GROUP
    shape = jax.ShapeDtypeStruct
    blocks = lambda width: pl.BlockSpec((WIDE_ROWS, width), lambda i: (i, 0))
    whole = lambda *dims: pl.BlockSpec(dims, lambda i: (0,) * len(dims))
    square = shape((2048, 128), f32)
    return pl.pallas_call(
        forward_kernel,
        grid=(steps,),
        in_specs=[
            pl.BlockSpec(memory_space=pltpu.SMEM),
            pl.BlockSpec(memory_space=pltpu.SMEM),
            pl.BlockSpec((WIDE_GROUP, 64, 1024), lambda i: (i, 0, 0)),
            pl.BlockSpec((WIDE_GROUP, 64, 1024), lambda i: (i, 0, 0)),
            whole(1, 1024),
        ]
        + [whole(256, 640)] * 4
        + [whole(4, 384)],
        out_specs=[blocks(1024), blocks(384), blocks(128), blocks(384)]
        + [blocks(128)] * 8
        + [pl.BlockSpec((1, WIDE_GROUP, 128), lambda i: (i, 0, 0))],
        out_shape=[
            shape((2048, 1024), bf16),
            shape((2048, 384), bf16),
            square,
            shape((2048, 384), f32),
        ]
        + [square] * 8
        + [shape((steps, WIDE_GROUP, 128), f32)],
        scratch_shapes=[
            pltpu.VMEM((128, 128), f32),
            pltpu.VMEM((WIDE_ROWS + 8, 384), f32),
            pltpu.VMEM((1024, 640), bf16),
        ],
        compiler_params=pltpu.CompilerParams(
            dimension_semantics=("arbitrary",), vmem_limit_bytes=VMEM_LIMIT
        ),
        cost_estimate=cost(30),
        name="delta_forward",
    )(numbers, places, mine, theirs, gain, *weights, taps)


def backward_kernel(
    numbers, places, taps, conv_in, cols_in, inv_in, from_in, upd_in, score_in, move_in, state_in, mixed_in,
    normed_in, heads_in, sq_mine, sq_theirs, in_mine, in_theirs, hidden_in, gate_in,
    weight_0, weight_1, weight_2, weight_3,
    head_in, keep_out, give_out, unit_out, low_out,
    after, ext, d_all, held, logits_out, taps_out, sums_out,
):
    step = pl.program_id(0)
    scale = numbers[2]

    @pl.when(step == 0)
    def _():
        after[...] = jnp.zeros_like(after)
        ext[ROWS : ROWS + 8, :] = jnp.zeros((8, 384), f32)
        taps_out[...] = jnp.zeros_like(taps_out)
        sums_out[...] = jnp.zeros_like(sums_out)
        unit_out[...] = jnp.zeros_like(unit_out)
        logits_out[...] = jnp.zeros_like(logits_out)
        for steps, weight in enumerate((weight_0, weight_1, weight_2, weight_3)):
            held[block_of(places, steps), :] = weight[...]

    rows, cols = square_iota()
    strict = cols < rows
    kept, maps = [], []
    for at in range(GROUP):
        here = slice(at * CHUNK, (at + 1) * CHUNK)
        q, k, rq, rk = unit_norms(silu(conv_in[here, :256]))
        queries, keys = q * (rq * 128**-0.5), k * rk
        column = cols_in[here, :]
        total = column[:, 2:3]
        growth = jnp.exp(total)
        last = total[CHUNK - 1 : CHUNK, :]
        rate = head_rates(sq_mine, sq_theirs, at)
        mean = row_to_square((in_mine[0, at : at + 1, :] + in_theirs[0, at : at + 1, :]) / 256.0)
        grads = split(rate * (normed_in[here, :] - heads_in[here, :] * (rate * rate * mean)))
        passed = dot3(split(score_in[here, :]), grads, TN)
        probe = stacked(split(growth * queries), split(-from_in[here, :]))
        added = dot3(probe, stacked(grads, split(passed)), TN)
        maps.append((split(move_in[here, :]), added))
        kept.append((queries, keys, rq, rk, grads, passed, column, growth, last))
    current = after[...]
    afters = [None] * GROUP
    for at in reversed(range(GROUP)):
        pair = split(current)
        afters[at] = (current, pair)
        current = dot3(maps[at][0], pair, TN) + maps[at][1]
    after[...] = current
    tri = jnp.where(cols >= rows, 1.0, 0.0).astype(bf16)
    tri3 = jnp.concatenate([tri, tri, tri], axis=1)
    scale_sum = jnp.zeros((CHUNK, CHUNK), f32)
    bias_sum = jnp.zeros((CHUNK, CHUNK), f32)
    for at in range(GROUP):
        here = slice(at * CHUNK, (at + 1) * CHUNK)
        queries, keys, rq, rk, grads, passed, column, growth, last = kept[at]
        beta = column[:, 0:1]
        total = column[:, 2:3]
        decay = decay_matrix(column, rows, cols)
        to_end = jnp.exp(last - total)
        keys_s = split(keys)
        state = state_in[here, :]
        state_s = split(state)
        later, later_s = afters[at]
        updates = split(upd_in[here, :])
        d_updates = passed + dot3(split(to_end * keys), later_s, NN)
        right = dot3(split(inv_in[here, :]), split(d_updates), TN)
        right_s = split(right)
        pair = stacked(grads, right_s)
        inner = dot3(pair, updates, NT)
        d_scores = split(inner[:CHUNK] * decay)
        d_lower = split(jnp.where(strict, -inner[CHUNK:] * decay, 0.0))
        through = dot3(pair, state_s, NT)
        k_end = to_end * dot3(updates, later_s, NT)
        d_pair = stacked(d_scores, d_lower)
        on_keys = dot3(d_pair, keys_s, NN)
        k_cols = dot3(d_pair, stacked(split(queries), split(beta * keys)), TN) + k_end
        d_queries = growth * through[:CHUNK] + on_keys[:CHUNK]
        k_rows = on_keys[CHUNK:] - growth * through[CHUNK:]
        k_beta = beta * k_rows
        d_keys = k_beta + k_cols
        values_conv = conv_in[here, 256:]
        values = silu(values_conv)
        d_beta = jnp.sum(keys * k_rows + right * values, axis=-1, keepdims=True)
        d_total = jnp.sum(queries * d_queries + keys * (k_beta - k_cols), axis=-1, keepdims=True)
        ends = jnp.sum(keys * k_end, axis=0, keepdims=True)
        ends = ends + jnp.exp(last) * jnp.sum(state * later, axis=0, keepdims=True)
        d_last = jnp.sum(ends, axis=1, keepdims=True)
        spread = jnp.broadcast_to(d_total, (CHUNK, CHUNK))
        d_glog = raw(tri3, jnp.concatenate(split3(spread), axis=0), NN) + d_last
        d_decay = -scale * d_glog * column[:, 3:4]
        scale_sum = scale_sum + d_glog * column
        bias_sum = bias_sum + d_decay
        d_all[here, 512:] = jnp.where(
            cols == 0, d_beta * beta * (1.0 - beta), jnp.where(cols == 1, d_decay, 0.0)
        ).astype(bf16)
        q_hat, k_hat = queries * 128**0.5, keys
        d_q = (rq * 128**-0.5) * (d_queries - q_hat * jnp.sum(q_hat * d_queries, axis=-1, keepdims=True))
        d_k = rk * (d_keys - k_hat * jnp.sum(k_hat * d_keys, axis=-1, keepdims=True))
        d_v = beta * right
        conv = conv_in[here, :]
        sig = jax.nn.sigmoid(conv)
        ext[here, :] = jnp.concatenate([d_q, d_k, d_v], axis=1) * (sig * (1.0 + conv * (1.0 - sig)))
    sums_out[0:1, :] += jnp.sum(scale_sum, axis=0, keepdims=True)
    sums_out[1:2, :] += jnp.sum(bias_sum, axis=0, keepdims=True)
    mixed = mixed_in[...].astype(f32)
    d_mixed = jnp.zeros((ROWS, 384), f32)
    for lag in range(CONV):
        moved = ext[CONV - 1 - lag : CONV - 1 - lag + ROWS, :]
        d_mixed = d_mixed + taps[lag : lag + 1, :] * moved
        taps_out[lag : lag + 1, :] += jnp.sum(mixed * moved, axis=0, keepdims=True)
    d_all[:, :384] = d_mixed.astype(bf16)
    d_all[:, 384:512] = gate_in[...]
    ext[ROWS : ROWS + 8, :] = ext[0:8, :]
    hidden = hidden_in[...]
    unit_out[...] += raw(hidden, d_all[:, :512], TN)
    logits_out[...] += raw(d_all[:, 512:], hidden, TN)[:8]
    first = numbers[0] < 0.5
    for at in range(GROUP):
        product = raw(d_all[at * CHUNK : (at + 1) * CHUNK, :], held[...], NT)
        low, high = product[:64], product[64:]
        keep_out[at] = jnp.where(first, low, high)
        give_out[at] = jnp.where(first, high, low).astype(bf16)

    @pl.when(step == 16 // GROUP - 1)
    def _():
        edge = [head_in[0:1, :], sums_out[0:2, :], jnp.zeros((1, 128), f32)]
        edge = jnp.concatenate([taps_out[0:4, :], jnp.concatenate(edge, axis=0)], axis=1)
        for grp in range(4):
            here = slice(grp * 256, grp * 256 + 256)
            low_out[grp, 0:256, :] = unit_out[here, :].astype(bf16)
            line = jnp.concatenate([logits_out[0:1, here], logits_out[1:2, here]], axis=1)
            small = jnp.concatenate([edge, line, jnp.zeros((3, 512), f32)], axis=0)
            low_out[grp, 256:272, :] = jnp.concatenate(split(small), axis=0)


def backward_call(numbers, places, taps, *arrays):
    steps = 16 // GROUP
    shape = jax.ShapeDtypeStruct
    blocks = lambda width: pl.BlockSpec((ROWS, width), lambda i: (steps - 1 - i, 0))
    halves = pl.BlockSpec((GROUP, 64, 1024), lambda i: (steps - 1 - i, 0, 0))
    lines = pl.BlockSpec((1, GROUP, 128), lambda i: (steps - 1 - i, 0, 0))
    whole = lambda *dims: pl.BlockSpec(dims, lambda i: (0,) * len(dims))
    return pl.pallas_call(
        backward_kernel,
        grid=(steps,),
        in_specs=[pl.BlockSpec(memory_space=pltpu.SMEM)] * 2
        + [whole(4, 384), blocks(384)]
        + [blocks(128)] * 7
        + [blocks(384), blocks(128), blocks(128)]
        + [lines] * 4
        + [blocks(1024), blocks(128)]
        + [whole(256, 640)] * 4
        + [whole(8, 128)],
        out_specs=[halves, halves, whole(1024, 512), whole(4, 272, 512)],
        out_shape=[
            shape((16, 64, 1024), f32),
            shape((16, 64, 1024), bf16),
            shape((1024, 512), f32),
            shape((4, 272, 512), bf16),
        ],
        scratch_shapes=[
            pltpu.VMEM((128, 128), f32),
            pltpu.VMEM((ROWS + 8, 384), f32),
            pltpu.VMEM((ROWS, 640), bf16),
            pltpu.VMEM((1024, 640), bf16),
            pltpu.VMEM((8, 1024), f32),
            pltpu.VMEM((8, 384), f32),
            pltpu.VMEM((8, 128), f32),
        ],
        compiler_params=pltpu.CompilerParams(
            dimension_semantics=("arbitrary",), vmem_limit_bytes=VMEM_LIMIT
        ),
        cost_estimate=cost(36),
        name="delta_backward",
    )(numbers, places, taps, *arrays)


def row_to_square(row):
    return jnp.broadcast_to(row, (CHUNK, CHUNK)).T


def head_rates(mine, theirs, at):
    squares = mine[0, at : at + 1, :] + theirs[0, at : at + 1, :]
    return row_to_square(lax.rsqrt(squares / 256.0 + epsilon))


def gate_kernel(heads, gate, mine, theirs, gain, out):
    for at in range(GROUP):
        here = slice(at * CHUNK, (at + 1) * CHUNK)
        normed = heads[here, :] * head_rates(mine, theirs, at)
        out[here, :] = (normed * gain[...] * silu(gate[here, :])).astype(bf16)


def specs(*widths):
    found = []
    for width in widths:
        if width == "rows":
            found.append(pl.BlockSpec((1, GROUP, 128), lambda i: (i, 0, 0)))
        elif width == "tokens":
            found.append(pl.BlockSpec((GROUP, 64, 1024), lambda i: (i, 0, 0)))
        elif width == "smem":
            found.append(pl.BlockSpec(memory_space=pltpu.SMEM))
        elif isinstance(width, tuple):
            found.append(pl.BlockSpec(width, lambda i, dims=len(width): (0,) * dims))
        else:
            found.append(pl.BlockSpec((ROWS, width), lambda i: (i, 0)))
    return found


def cost(microseconds):
    return pl.CostEstimate(flops=microseconds * 10**9, bytes_accessed=microseconds * 3 * 10**6, transcendentals=0)


def params():
    return pltpu.CompilerParams(dimension_semantics=("arbitrary",), vmem_limit_bytes=VMEM_LIMIT)


def gate_call(heads, gate, mine, theirs, gain):
    return pl.pallas_call(
        gate_kernel,
        grid=(16 // GROUP,),
        in_specs=specs(128, 128, "rows", "rows", (1, 128)),
        out_specs=specs(128)[0],
        out_shape=jax.ShapeDtypeStruct((2048, 128), bf16),
        compiler_params=params(),
        cost_estimate=cost(3),
        name="gate",
    )(heads, gate, mine, theirs, gain)


def middle_kernel(places, gated, tokens, *refs):
    weights, (gain, middle_out, hidden_out) = refs[:8], refs[8:]
    core = places[0]
    for at in range(2):
        line = tokens[at].astype(f32)
        for side, parity in enumerate((core, 1 - core)):
            for grp in range(4):
                first = at * 16 + places[2 + grp] * 4 + parity * 2
                found = jnp.concatenate([gated[first], gated[first + 1]], axis=1)
                line = line + raw(found, weights[side * 4 + grp][...], NN)
        rows = slice(at * 64, at * 64 + 64)
        middle_out[rows, :] = line
        rate = lax.rsqrt(jnp.mean(line * line, axis=-1, keepdims=True) + epsilon)
        hidden_out[rows, :] = (line * rate * gain[...]).astype(bf16)


def middle_call(places, gated, tokens, mine, theirs, gain):
    shape = jax.ShapeDtypeStruct
    return pl.pallas_call(
        middle_kernel,
        in_specs=[pl.BlockSpec(memory_space=pltpu.SMEM)] + [pl.BlockSpec(memory_space=pltpu.VMEM)] * 11,
        out_shape=[shape((128, 1024), f32), shape((128, 1024), bf16)],
        compiler_params=pltpu.CompilerParams(vmem_limit_bytes=VMEM_LIMIT),
        cost_estimate=cost(4),
        name="middle",
    )(places, gated, tokens, *mine, *theirs, gain)


def d_gated_kernel(places, grads, *refs):
    weights, out = refs[:8], refs[8]
    core = places[0]
    for side, parity in enumerate((core, 1 - core)):
        for grp in range(4):
            found = raw(grads[...], weights[side * 4 + grp][...], NT)
            for seq in range(2):
                for half in range(2):
                    to = seq * 16 + places[2 + grp] * 4 + parity * 2 + half
                    out[to] = found[seq * 64 : seq * 64 + 64, half * 128 : half * 128 + 128]


def d_gated_call(places, grads, mine, theirs):
    return pl.pallas_call(
        d_gated_kernel,
        in_specs=[pl.BlockSpec(memory_space=pltpu.SMEM)] + [pl.BlockSpec(memory_space=pltpu.VMEM)] * 9,
        out_shape=jax.ShapeDtypeStruct((32, 64, 128), f32),
        compiler_params=pltpu.CompilerParams(vmem_limit_bytes=VMEM_LIMIT),
        cost_estimate=cost(3),
        name="d_gated",
    )(places, grads, *mine, *theirs)


def output_weights_kernel(
    left_0, left_1, left_2, left_3, grads_0, grads_1, grads_2, grads_3, out
):
    grads = jnp.concatenate([grads_0[...], grads_1[...], grads_2[...], grads_3[...]], axis=0)
    for parity in range(2):
        for half in range(2):
            left = [side[seq, parity, half] for side in (left_0, left_1, left_2, left_3) for seq in range(2)]
            found = raw(jnp.concatenate(left, axis=0), grads, TN).astype(bf16)
            for part in range(8):
                for block in range(8):
                    piece = found[part * 16 : part * 16 + 16, block * 128 : block * 128 + 128]
                    at = parity * 128 + block * 16
                    out[half * 8 + part, at : at + 16, :] = piece


def output_weights_call(*arrays):
    return pl.pallas_call(
        output_weights_kernel,
        in_specs=[pl.BlockSpec(memory_space=pltpu.VMEM)] * 8,
        out_shape=jax.ShapeDtypeStruct((16, 256, 128), bf16),
        compiler_params=pltpu.CompilerParams(vmem_limit_bytes=VMEM_LIMIT),
        cost_estimate=cost(3),
        name="output_weights",
    )(*arrays)


def ff_kernel(two, dy, weight, down, swi_out, grads_out, part_out):
    gateup = raw(two[...], weight[...], NN)
    d_swi = raw(dy[...], down[...], NT)
    gate, up = gateup[:, :384], gateup[:, 384:]
    sig = jax.nn.sigmoid(gate)
    active = gate * sig
    swi_out[...] = (active * up).astype(bf16)
    grads_out[:, :384] = (d_swi * up * (sig * (1.0 + gate * (1.0 - sig)))).astype(bf16)
    grads_out[:, 384:] = (d_swi * active).astype(bf16)
    part_out[...] = raw(grads_out[...], weight[...], NT)


def ff_call(two, dy, weight, down):
    shape = jax.ShapeDtypeStruct
    rows = lambda width: pl.BlockSpec((256, width), lambda i: (i, 0))
    whole = lambda *dims: pl.BlockSpec(dims, lambda i: (0, 0))
    return pl.pallas_call(
        ff_kernel,
        grid=(2,),
        in_specs=[rows(1024), rows(1024), whole(1024, 768), whole(384, 1024)],
        out_specs=[rows(384), rows(768), rows(1024)],
        out_shape=[shape((512, 384), bf16), shape((512, 768), bf16), shape((512, 1024), f32)],
        compiler_params=params(),
        cost_estimate=cost(5),
        name="ff",
    )(two, dy, weight, down)


def ff_sum_kernel(two, dy, weight, down, added, swi_out, grads_out, low_out, own_out, part):
    ff_kernel(two, dy, weight, down, swi_out, grads_out, part)
    total = part[...] + added[...]
    low_out[...] = total.astype(bf16)

    @pl.when(pl.program_id(0) == 0)
    def _():
        own_out[...] = total[:128]


def ff_sum_call(two, dy, weight, down, added):
    shape = jax.ShapeDtypeStruct
    rows = lambda width: pl.BlockSpec((256, width), lambda i: (i, 0))
    whole = lambda *dims: pl.BlockSpec(dims, lambda i: (0, 0))
    return pl.pallas_call(
        ff_sum_kernel,
        grid=(2,),
        in_specs=[rows(1024), rows(1024), whole(1024, 768), whole(384, 1024), rows(1024)],
        out_specs=[rows(384), rows(768), rows(1024), whole(128, 1024)],
        out_shape=[
            shape((512, 384), bf16),
            shape((512, 768), bf16),
            shape((512, 1024), bf16),
            shape((128, 1024), f32),
        ],
        scratch_shapes=[pltpu.VMEM((256, 1024), f32)],
        compiler_params=params(),
        cost_estimate=cost(5),
        name="ff_sum",
    )(two, dy, weight, down, added)


def gate_back_kernel(
    d_gated, heads, gate, sq_mine, sq_theirs, gain,
    normed_out, gate_out, inner_out, head_out,
):
    @pl.when(pl.program_id(0) == 0)
    def _():
        head_out[...] = jnp.zeros_like(head_out)

    ones = jnp.ones((8, 256), bf16)
    for at in range(GROUP):
        here = slice(at * CHUNK, (at + 1) * CHUNK)
        grads = d_gated[here, :]
        value = heads[here, :]
        normed = value * head_rates(sq_mine, sq_theirs, at)
        logits = gate[here, :]
        sig = jax.nn.sigmoid(logits)
        active = logits * sig
        head_out[0:1, :] += jnp.sum(grads * normed * active, axis=0, keepdims=True)
        gained = grads * gain[...]
        gate_out[here, :] = (gained * normed * (sig * (1.0 + logits * (1.0 - sig)))).astype(bf16)
        d_normed = gained * active
        normed_out[here, :] = d_normed
        product = raw(ones, jnp.concatenate(split(d_normed * value), axis=1), NT)
        inner_out[0, at : at + 1, :] = product[0:1, :]


def gate_back_call(*arrays):
    shape = jax.ShapeDtypeStruct
    return pl.pallas_call(
        gate_back_kernel,
        grid=(16 // GROUP,),
        in_specs=specs(128, 128, 128, "rows", "rows", (1, 128)),
        out_specs=specs(128, 128, "rows", (8, 128)),
        out_shape=[
            shape((2048, 128), f32),
            shape((2048, 128), bf16),
            shape((16 // GROUP, GROUP, 128), f32),
            shape((8, 128), f32),
        ],
        compiler_params=params(),
        cost_estimate=cost(4),
        name="gate_back",
    )(*arrays)


def ff_weights_kernel(two_0, two_1, grads_0, grads_1, swi_0, swi_1, dy_0, dy_1, out):
    grp = pl.program_id(0)
    found = raw(two_0[...], grads_0[...], TN) + raw(two_1[...], grads_1[...], TN)
    for chip in range(16):
        for part in range(6):
            at = pl.multiple_of(grp * 96 + part * 16, 16)
            block = found[chip * 16 : chip * 16 + 16, part * 128 : part * 128 + 128]
            out[chip, pl.ds(at, 16), :] = block
    found = raw(swi_0[...], dy_0[...], TN) + raw(swi_1[...], dy_1[...], TN)
    for chip in range(16):
        for part in range(2):
            at = pl.multiple_of(384 + grp * 64 + part * 32, 32)
            if chip < 11:
                block = found[chip * 32 : chip * 32 + 32, part * 128 : part * 128 + 128]
            else:
                block = jnp.zeros((32, 128), f32)
            out[chip, pl.ds(at, 32), :] = block


def ff_weights_call(*arrays):
    columns = pl.BlockSpec((512, 256), lambda i: (0, i))
    whole = lambda width: pl.BlockSpec((512, width), lambda i: (0, 0))
    return pl.pallas_call(
        ff_weights_kernel,
        grid=(4,),
        in_specs=[columns] * 2 + [whole(768)] * 2 + [whole(384)] * 2 + [columns] * 2,
        out_specs=pl.BlockSpec((16, 640, 128), lambda i: (0, 0, 0)),
        out_shape=jax.ShapeDtypeStruct((16, 640, 128), f32),
        compiler_params=params(),
        cost_estimate=cost(7),
        name="ff_weights",
    )(*arrays)


def ff_grads_kernel(numbers, places, mine, theirs, weight, gain, gateup_out, down_out, output_out, gain_out):
    step = pl.program_id(0)
    first = numbers[0] < 0.5

    def piece(core, chip, at, size):
        one, two = mine[chip, pl.ds(at, size), :], theirs[chip, pl.ds(at, size), :]
        return (jnp.where(first, one, two) if core == 0 else jnp.where(first, two, one)).astype(f32)

    for chip in range(4):
        rows = slice(chip * 16, chip * 16 + 16)
        total = jnp.zeros((16, 128), f32)
        for half in range(2):
            found = []
            for grp in range(4):
                for core in range(2):
                    for part in range(3):
                        at = pl.multiple_of(places[2 + grp] * 96 + half * 48 + part * 16, 16)
                        block = piece(core, chip, at, 16)
                        found.append(block if part < 2 else block[:, :96])
            line = jnp.concatenate(found, axis=1)
            gateup_out[rows, half * FF : (half + 1) * FF] = line
            product = line * weight[rows, half * FF : (half + 1) * FF].astype(f32)
            for part in range(FF // 128):
                total = total + product[:, part * 128 : part * 128 + 128]
        total = jnp.sum(total, axis=1, keepdims=True)
        gain_out[rows, :] = jnp.broadcast_to(total, (16, 128)) / gain[rows, :].astype(f32)

        for core in range(2):
            at = pl.multiple_of(core * 256 + (step * 4 + chip) * 16, 16)
            for part in range(8):
                output_out[pl.ds(at, 16), part * 128 : part * 128 + 128] = piece(core, chip, 640 + part * 16, 16)

        @pl.when(step * 4 + chip < 11)
        def _():
            for core in range(2):
                at = pl.multiple_of(core * 352 + (step * 4 + chip) * 32, 8)
                for part in range(8):
                    down_out[pl.ds(at, 32), part * 128 : part * 128 + 128] = piece(core, chip, 384 + part * 32, 32)


def ff_grads_call(numbers, places, mine, theirs, weight, gain):
    shape = jax.ShapeDtypeStruct
    return pl.pallas_call(
        ff_grads_kernel,
        grid=(4,),
        in_specs=[
            pl.BlockSpec(memory_space=pltpu.SMEM),
            pl.BlockSpec(memory_space=pltpu.SMEM),
            pl.BlockSpec((4, 768, 128), lambda i: (i, 0, 0)),
            pl.BlockSpec((4, 768, 128), lambda i: (i, 0, 0)),
            pl.BlockSpec((64, 2 * FF), lambda i: (i, 0)),
            pl.BlockSpec((64, 128), lambda i: (i, 0)),
        ],
        out_specs=[
            pl.BlockSpec((64, 2 * FF), lambda i: (i, 0)),
            pl.BlockSpec((704, 1024), lambda i: (0, 0)),
            pl.BlockSpec((512, 1024), lambda i: (0, 0)),
            pl.BlockSpec((64, 128), lambda i: (i, 0)),
        ],
        out_shape=[
            shape((256, 2 * FF), f32),
            shape((704, 1024), f32),
            shape((512, 1024), f32),
            shape((256, 128), f32),
        ],
        compiler_params=params(),
        cost_estimate=cost(8),
        name="ff_grads",
    )(numbers, places, mine, theirs, weight, gain)


def mixer_grads_kernel(numbers, mine, theirs, weight, gate_weight, mixer_out, gate_out, sum_out):
    first = numbers[0] < 0.5
    for head in range(8):
        one, two = mine[head], theirs[head]
        for core in range(2):
            piece = jnp.where(first, one, two) if core == 0 else jnp.where(first, two, one)
            piece = piece.astype(f32)
            rows = slice(core * 64, core * 64 + 64)
            mixer_out[rows, head * 128 : head * 128 + 128] = piece[:64]
            mixer_out[rows, 1024 + head * 128 : 1152 + head * 128] = piece[64:128]
            to = 2048 + head * 256 + core * 128
            mixer_out[:, to : to + 128] = piece[128:256]
            to = head * 256 + core * 128
            gate_out[:, to : to + 128] = piece[256:384]
    total = jnp.sum(mixer_out[...] * weight[...].astype(f32), axis=1, keepdims=True)
    total = total + jnp.sum(gate_out[...] * gate_weight[...].astype(f32), axis=1, keepdims=True)
    sum_out[...] = jnp.broadcast_to(total, (128, 128))


def mixer_grads_call(numbers, mine, theirs, weight, gate_weight):
    shape = jax.ShapeDtypeStruct
    return pl.pallas_call(
        mixer_grads_kernel,
        grid=(2,),
        in_specs=[
            pl.BlockSpec(memory_space=pltpu.SMEM),
            pl.BlockSpec((8, 384, 128), lambda i: (i, 0, 0)),
            pl.BlockSpec((8, 384, 128), lambda i: (i, 0, 0)),
            pl.BlockSpec((128, 4096), lambda i: (i, 0)),
            pl.BlockSpec((128, 2048), lambda i: (i, 0)),
        ],
        out_specs=[
            pl.BlockSpec((128, 4096), lambda i: (i, 0)),
            pl.BlockSpec((128, 2048), lambda i: (i, 0)),
            pl.BlockSpec((128, 128), lambda i: (i, 0)),
        ],
        out_shape=[shape((256, 4096), f32), shape((256, 2048), f32), shape((256, 128), f32)],
        compiler_params=params(),
        cost_estimate=cost(4),
        name="mixer_grads",
    )(numbers, mine, theirs, weight, gate_weight)


def mm(left, right):
    return raw(left, right, NN)


def mm_t(left, right):
    return raw(left, right, NT)


def t_mm(left, right):
    return raw(left, right, TN)


def other_core(value):
    return lax.ppermute(value, "ctx", OTHER_CORE)


def other_seq(value):
    return lax.ppermute(value, "ctx", OTHER_SEQ)


def along_grp(value, steps):
    return lax.ppermute(value, "grp", [(at, (at + steps) % 4) for at in range(4)])


def from_grp(value):
    return [value] + [along_grp(value, steps) for steps in (1, 2, 3)]


def in_grp_order(pieces, place):
    turned = [pieces[0], pieces[3], pieces[2], pieces[1]]
    doubled = jnp.stack(turned + turned[:3])
    return lax.dynamic_slice_in_dim(doubled, (4 - place) % 4, 4, axis=0)


def exchange_grp(value, place):
    part = lambda steps: lax.dynamic_index_in_dim(value, (place + steps) % 4, 0, False)
    return [part(0)] + [along_grp(part(steps), steps) for steps in (1, 2, 3)]


def sum_grp(value, place):
    mine, *others = exchange_grp(value.astype(bf16), place)
    total = lax.dynamic_index_in_dim(value, place, 0, False)
    for other in others:
        total = total + other.astype(f32)
    return total


def sum_chips(value):
    flat = value.reshape(-1, 128)
    return lax.psum_scatter(flat, "ctx", scatter_dimension=0, tiled=True, axis_index_groups=CHIPS)


def wide_columns(value):
    return jnp.concatenate([value[:, at * 128 : at * 128 + 128] for at in range(4)], axis=0)


def over_chips(value):
    return lax.all_to_all(value, "ctx", 0, 0, axis_index_groups=CHIPS)


def body(
    block_input,
    seq_lengths,
    in_gain,
    w_mixer,
    conv_weight,
    w_rates,
    decay_scale,
    decay_bias,
    w_outgate,
    head_gain,
    w_output,
    mlp_gain,
    w_gateup,
    w_down,
    cotangent,
):
    place = lax.axis_index("ctx")
    grp = lax.axis_index("grp")
    core = place % 2
    head = (place % 16) // 2
    seq = place // 16
    unit = place % 16

    x_all = jnp.repeat(block_input, 8, axis=0)
    w_mixer_one, w_output_one, x_all = lax.optimization_barrier((w_mixer, w_output, x_all))
    x_mine = over_chips(x_all)

    def unit_columns(value):
        q_part = lax.dynamic_slice_in_dim(value, head * 128, 128, axis=1)
        k_part = lax.dynamic_slice_in_dim(value, 1024 + head * 128, 128, axis=1)
        v_part = lax.dynamic_slice_in_dim(value, 2048 + unit * 128, 128, axis=1)
        return [q_part, k_part, v_part]

    small = jnp.concatenate(
        [
            conv_weight.reshape(-1),
            in_gain,
            mlp_gain,
            head_gain,
            decay_scale,
            decay_bias,
            jnp.zeros((188,), bf16),
        ]
    ).reshape(256, 19)
    unit_part = jnp.concatenate(
        unit_columns(w_mixer_one)
        + [
            lax.dynamic_slice_in_dim(w_outgate, unit * 128, 128, axis=1),
            lax.dynamic_slice_in_dim(w_rates, head, 1, axis=1),
            lax.dynamic_slice_in_dim(w_rates, 8 + head, 1, axis=1),
            small,
            jnp.zeros((256, 107), bf16),
        ],
        axis=1,
    )
    w_unit = from_grp(unit_part)
    small = in_grp_order([piece[:, 514:533] for piece in w_unit], grp).reshape(4, -1)
    conv_full = small[:, :4096].reshape(4, 4, 1024).transpose(1, 0, 2).reshape(4, 4096).astype(f32)
    gain_one = small[:, 4096:4352].reshape(1, 1024).astype(f32)
    gain_two = small[:, 4352:4608].reshape(1, 1024).astype(f32)
    head_full = small[:, 4608:4672].reshape(1, 256).astype(f32)
    scale_full = small[:, 4672:4674].reshape(8).astype(f32)
    bias_full = small[:, 4674:4676].reshape(8).astype(f32)

    taps = jnp.concatenate(unit_columns(conv_full), axis=1)
    scale = lax.dynamic_index_in_dim(scale_full, head, 0, False)
    bias = lax.dynamic_index_in_dim(bias_full, head, 0, False)
    head_half = lax.dynamic_slice_in_dim(head_full, core * 128, 128, axis=1)
    numbers = jnp.stack([core.astype(f32), bias, jnp.exp(scale), jnp.zeros((), f32)])

    def ff_columns(owner):
        at = owner * 704 + core * 352
        gate = lax.dynamic_slice_in_dim(w_gateup, at, 352, axis=1)
        up = lax.dynamic_slice_in_dim(w_gateup, FF + at, 352, axis=1)
        fill = jnp.zeros((256, 32), bf16)
        return jnp.concatenate([gate, fill, up, fill], axis=1)

    gateup_pieces = jnp.stack([ff_columns(owner) for owner in range(4)])
    w_dn = jnp.concatenate(
        [lax.dynamic_slice_in_dim(w_down, core * 352, 352, axis=0), jnp.zeros((32, 1024), bf16)], axis=0
    )
    output_half = lax.dynamic_slice_in_dim(w_output_one, core * 256, 256, axis=0)

    positions = place * 64 + lax.broadcasted_iota(jnp.int32, (2, 64), 1)
    valid = (positions < seq_lengths[:, None]).astype(f32)[..., None]
    inputs_rows = block_input.astype(f32).reshape(128, 1024)
    r_one = lax.rsqrt(jnp.mean(inputs_rows * inputs_rows, axis=-1, keepdims=True) + epsilon)
    dy = (cotangent.astype(f32) * valid).reshape(128, 1024)
    dy_low = dy.astype(bf16)

    def to_wide(tokens):
        mine = jnp.concatenate(from_grp(tokens), axis=0)
        return mine, other_core(mine)

    def over_cores(mine, theirs, sent):
        mine = mine + other_core(theirs.astype(sent)).astype(f32)
        return mine[:128], mine.reshape(4, 128, 1024).astype(bf16)

    def over_grp(total, low):
        for steps in (1, 2, 3):
            total = total + along_grp(low[steps], -steps).astype(f32)
        return total

    places = jnp.stack([core, head] + [(grp - steps) % 4 for steps in range(4)])
    output_pieces = from_grp(output_half)
    gateup_pieces, w_dn, w_unit, output_pieces, numbers, places, gain_one, taps, x_mine = lax.optimization_barrier(
        (gateup_pieces, w_dn, w_unit, output_pieces, numbers, places, gain_one, taps, x_mine)
    )
    x_theirs = other_core(x_mine)
    gateup_pieces = lax.all_to_all(gateup_pieces, "grp", 0, 0)
    (
        hidden_one, mixed_in, outgate, conv, columns, inverse, from_state, updates, scores, moves, states, heads_out,
        squares,
    ) = forward_call(numbers, places, x_mine, x_theirs, gain_one, w_unit, taps)
    heads_out, squares, gateup_pieces = lax.optimization_barrier((heads_out, squares, gateup_pieces))
    squares = squares.reshape(16 // GROUP, GROUP, 128)
    squares_theirs = other_core(squares)
    gated = gate_call(heads_out, outgate, squares, squares_theirs, head_half)

    dy_low, output_pieces, gated = lax.optimization_barrier((dy_low, output_pieces, gated))
    gated_tokens = lax.all_to_all(gated.reshape(32, 64, 128), "ctx", 0, 0)
    output_theirs = [other_core(piece) for piece in output_pieces]
    dy_pieces = from_grp(dy_low)
    middle, hidden_two = middle_call(places, gated_tokens, block_input, output_pieces, output_theirs, gain_two)
    r_two = lax.rsqrt(jnp.mean(middle * middle, axis=-1, keepdims=True) + epsilon)
    dy_pieces, hidden_two = lax.optimization_barrier((dy_pieces, hidden_two))
    dy_mine = jnp.concatenate(dy_pieces, axis=0)
    dy_theirs = other_core(dy_mine)
    two_mine, two_theirs = to_wide(hidden_two)
    w_gu = gateup_pieces.reshape(1024, 768)
    swi_theirs, grads_theirs, part_theirs = ff_call(two_theirs, dy_theirs, w_gu, w_dn)
    by_grp = exchange_grp(gated_tokens.reshape(2, 4, 2, 2, 64, 128).transpose(1, 0, 2, 3, 4, 5), grp)
    swi_mine, grads_mine, part_low, part_own = ff_sum_call(two_mine, dy_mine, w_gu, w_dn, other_core(part_theirs))
    part_low, part_own, swi_mine, grads_mine, by_grp = lax.optimization_barrier(
        (part_low, part_own, swi_mine, grads_mine, by_grp)
    )
    g_ff = ff_weights_call(
        two_mine, two_theirs, grads_mine, grads_theirs, swi_mine, swi_theirs, dy_mine, dy_theirs
    )
    dhidden_two = over_grp(part_own, part_low.reshape(4, 128, 1024))
    scaled = dhidden_two * gain_two
    dmiddle = dy + r_two * scaled - middle * r_two**3 * jnp.mean(scaled * middle, axis=-1, keepdims=True)
    dmix = dmiddle.astype(bf16)
    dmix, g_ff = lax.optimization_barrier((dmix, g_ff))
    g_ff = sum_chips(g_ff)
    d_gated = d_gated_call(places, dmix, output_pieces, output_theirs)
    dmix, d_gated = lax.optimization_barrier((dmix, d_gated))
    d_gated = lax.all_to_all(d_gated, "ctx", 0, 0)

    dmix_pieces, d_gated = lax.optimization_barrier((from_grp(dmix), d_gated))
    g_output = output_weights_call(*by_grp, *dmix_pieces)
    d_gated, g_output = lax.optimization_barrier((d_gated, g_output))
    g_output = over_chips(g_output)

    d_normed, d_outgate, inner, g_head = gate_back_call(
        d_gated.reshape(2048, 128), heads_out, outgate, squares, squares_theirs, head_half
    )
    inner_theirs = other_core(inner)
    keep, give, g_unit, g_unit_low = backward_call(
        numbers, places, taps, conv, columns, inverse, from_state, updates, scores, moves, states, mixed_in,
        d_normed, heads_out, squares, squares_theirs, inner, inner_theirs, hidden_one, d_outgate, *w_unit, g_head,
    )

    give, g_output = lax.optimization_barrier((give, g_output))
    give_theirs = other_core(give)
    d_sent = (keep + give_theirs.astype(f32)).astype(bf16)
    g_ff, g_output, g_unit_low, d_sent = lax.optimization_barrier((g_ff, g_output, g_unit_low, d_sent))
    d_tokens = over_chips(d_sent)
    g_unit_pieces = exchange_grp(g_unit_low, grp)
    g_output = g_output.astype(f32).sum(axis=0).reshape(2, 128, 128)
    g_output_theirs = other_core(lax.dynamic_index_in_dim(g_output, 1 - core, 0, False).astype(bf16))
    g_output = lax.dynamic_index_in_dim(g_output, core, 0, False) + g_output_theirs.astype(f32)
    g_gu = exchange_grp(g_ff[:384].astype(bf16).reshape(4, 96, 128), grp)
    early = jnp.concatenate(g_gu + [g_ff[384:].astype(bf16), g_output.astype(bf16)], axis=0)
    g_unit_pieces, d_tokens = lax.optimization_barrier((g_unit_pieces, d_tokens))
    early_mine = lax.all_gather(early, "ctx", axis_index_groups=CHIPS)
    early_theirs = other_core(early_mine)
    grad_gateup, grad_down, grad_output, mlp_sums = ff_grads_call(
        numbers, places, early_mine, early_theirs, w_gateup, jnp.broadcast_to(mlp_gain[:, None], (256, 128))
    )

    g_small = sum(piece[256:264].astype(f32) + piece[264:].astype(f32) for piece in g_unit_pieces)
    g_sum = lax.dynamic_index_in_dim(g_unit.reshape(4, 256, 512), grp, 0, False)
    for other in g_unit_pieces[1:]:
        g_sum = g_sum + other[:256].astype(f32)
    g_sum = g_sum.reshape(2, 128, 512)

    dhidden_one = d_tokens.astype(f32)
    dhidden_one = dhidden_one.reshape(2, 8, 64, 1024).sum(axis=1).reshape(128, 1024)
    scaled = dhidden_one * gain_one
    input_grad = (
        dmiddle + r_one * scaled - inputs_rows * r_one**3 * jnp.mean(scaled * inputs_rows, axis=-1, keepdims=True)
    )

    mine = lax.dynamic_index_in_dim(g_sum, seq, 0, False)
    given = lax.dynamic_index_in_dim(g_sum, 1 - seq, 0, False).astype(bf16)
    mine = mine + other_seq(given).astype(f32)
    halves = mine[:, :256].reshape(2, 64, 256)
    qk_mine = lax.dynamic_index_in_dim(halves, core, 0, False)
    qk_given = lax.dynamic_index_in_dim(halves, 1 - core, 0, False).astype(bf16)
    qk_mine = qk_mine + other_core(qk_given).astype(f32)
    late = [qk_mine[:, :128], qk_mine[:, 128:], mine[:, 256:384], mine[:, 384:]]
    late = jnp.concatenate(late, axis=0).astype(bf16)
    small_high = lax.optimization_barrier(g_small.astype(bf16))
    small_low = (g_small - small_high.astype(f32)).astype(bf16)
    late = jnp.concatenate([late, wide_columns(small_high), wide_columns(small_low)], axis=0)
    late, swi_mine, swi_theirs = lax.optimization_barrier((late, swi_mine, swi_theirs))
    late_mine = over_chips(jnp.broadcast_to(late, (16,) + late.shape))
    block_out = middle + over_grp(*over_cores(mm(swi_mine, w_dn), mm(swi_theirs, w_dn), bf16))
    block_output = (block_out.reshape(2, 64, 1024) * valid).astype(bf16)
    late_mine, block_output, input_grad = lax.optimization_barrier((late_mine, block_output, input_grad))
    late_theirs = other_core(late_mine)
    grad_mixer, grad_outgate, mixer_sums = mixer_grads_call(numbers, late_mine, late_theirs, w_mixer, w_outgate)
    small_of = lambda found: (found[:, 384:416].astype(f32) + found[:, 416:448].astype(f32)).reshape(2, 8, 32, 128).sum(axis=0)
    small_one, small_two = small_of(late_mine), small_of(late_theirs)
    small_low, small_high = jnp.where(core == 0, small_one, small_two), jnp.where(core == 0, small_two, small_one)
    both = small_one + small_two
    taps_q = both[:, 0:4].transpose(1, 0, 2).reshape(4, 1024)
    taps_k = both[:, 8:12].transpose(1, 0, 2).reshape(4, 1024)
    taps_v = jnp.stack([small_low[:, 16:20], small_high[:, 16:20]], axis=1).transpose(2, 0, 1, 3).reshape(4, 2048)
    grad_conv = jnp.concatenate([taps_q, taps_k, taps_v], axis=1)
    grad_conv = lax.dynamic_slice_in_dim(grad_conv, grp * 1024, 1024, axis=1)
    grad_head = jnp.concatenate([small_low[:, 24].sum(axis=0), small_high[:, 24].sum(axis=0)])
    grad_head = lax.dynamic_slice_in_dim(grad_head, grp * 64, 64, axis=0)
    grad_scale = lax.dynamic_slice_in_dim(both[:, 25, 1], grp * 2, 2, axis=0)
    grad_bias = lax.dynamic_slice_in_dim(both[:, 26, 1], grp * 2, 2, axis=0)
    rates = jnp.stack([both[:, 4], both[:, 12], both[:, 20], both[:, 28]], axis=1)
    grad_rates = rates.reshape(8, 2, 256).transpose(1, 0, 2).reshape(16, 256).T
    grad_in_gain = (
        mixer_sums[:, 0]
        + jnp.sum(grad_rates * w_rates.astype(f32), axis=1)
    ) / in_gain.astype(f32)

    return (
        block_output,
        input_grad.reshape(2, 64, 1024),
        grad_in_gain,
        grad_mixer,
        grad_conv,
        grad_rates,
        grad_scale,
        grad_bias,
        grad_outgate,
        grad_head,
        grad_output,
        mlp_sums[:, 0],
        grad_gateup,
        grad_down,
    )


def solution(mesh):
    tokens = P("grp", "ctx", None)
    rows = P("grp", None)
    one = P("grp")
    taps = P(None, "grp")
    return jax.shard_map(
        body,
        mesh=mesh,
        in_specs=(tokens, one, one, rows, taps, rows, one, one, rows, one, rows, one, rows, rows, tokens),
        out_specs=(tokens, tokens, one, rows, taps, rows, one, one, rows, one, rows, one, rows, rows),
        check_vma=False,
    )
```
